256 devices in a mesh: dp: 32 (over x, z), mp: 8 (over y, core).
Axes of the slice: x: 4, y: 4, z: 8, core: 2. Of those that a mesh axis runs over, the one named last changes fastest.
Arguments:
- tiles: bfloat16 [512, 8, 3200], P('dp', None, 'mp'), may hold values from -6 to 6
- tile_counts: int32 [64], replicated, may hold values from 5 to 8, as said below
- encoder_rank: int32 [512], replicated, may hold values from 0 to 31, as said below
- out_grad: bfloat16 [512, 8, 3200], P('dp', None, 'mp'), may hold values from -6 to 6
- norm_gain: float32 [3200], replicated, may hold values from 0.5 to 1.5
- layer_scale: float32 [3200], replicated, may hold values from 0.4 to 1.6
- up_weight: bfloat16 [3200, 6400], P(None, 'mp'), may hold values from -0.109375 to 0.109375
- down_weight: bfloat16 [3200, 6400], P(None, 'mp'), may hold values from -0.078125 to 0.078125
Outputs:
- embedded: bfloat16 [512, 8, 3200], P('dp', None, 'mp')
- tile_grads: bfloat16 [512, 8, 3200], P('dp', None, 'mp')
- weight_grads: bfloat16 [3200, 6400], P('dp', 'mp')
The draws below stay inside these ranges and needn't reach their ends.
Inputs may be any that keep to these rules, and one draw needn't show every extreme that they name: Sample i's tiles occupy the first tile_counts[i] of its 8 slots; some sample has exactly 8 tiles. `encoder_rank`: among live slots, no data rank sends two tiles to the same encoder rank; every encoder rank receives at most 16 live tiles and some encoder rank receives exactly 16.
All inputs are finite; a program needn't handle non-finite values.
Results may differ from the reference program's by a relative error of at most 0.029.
Values may be sent and summed in bfloat16 or wider, within the bound.
A program may use at most 64 MiB of HBM per device.

```python
import jax
import jax.numpy as jnp
from jax import lax

D = 3200
FF = 6400
MAXT = 8
ROWS = 8
SAMP_DEV = 2
SLOTS = 16
TILES = 512
N_DP = 32


def tile_plan(key):
    key_counts, key_offsets, key_target = jax.random.split(key, 3)
    counts = jax.random.randint(key_counts, (N_DP * SAMP_DEV,), 5, MAXT + 1)
    shuffled = jax.random.permutation(key_offsets, N_DP)
    place_ids = jnp.arange(N_DP)
    score = jnp.where(shuffled == 1, -2, jnp.where(shuffled == N_DP // 2, -1, place_ids))
    offsets = shuffled[jnp.argsort(score, stable=True)][:SLOTS]
    target = jax.random.randint(key_target, (), 0, N_DP)
    slot_index = jnp.arange(SLOTS)
    sources = (target - offsets) % N_DP
    forced = sources * SAMP_DEV + slot_index // MAXT
    needed = slot_index % MAXT + 1
    counts = counts.at[forced].max(needed)
    senders = jnp.arange(N_DP)
    dest_table = (senders[:, None] + offsets[None, :]) % N_DP
    return (counts.astype(jnp.int32), dest_table.reshape(-1).astype(jnp.int32))


def draw_tile_counts(key, part):
    return tile_plan(key)[0]


def draw_encoder_rank(key, part):
    return tile_plan(key)[1]


def shard_levels(own_key, shape, cuts, least, top_value):
    def one(axis_at, parts):
        heights = jax.random.uniform(jax.random.fold_in(jax.random.fold_in(own_key, 6), axis_at), (parts,), jnp.float32, least / len(cuts), top_value / len(cuts))
        return jnp.repeat(jnp.exp(heights), shape[axis_at] // parts).reshape((-1,) + (1,) * (len(shape) - axis_at - 1))

    gain = one(*cuts[0])
    for cut in cuts[1:]:
        gain = gain * one(*cut)
    return gain


def normal_values(stream_key, shape, width, most, cuts=(), kind=jnp.bfloat16):
    entries = jax.random.normal(stream_key, shape, jnp.float32) * width
    if len(cuts) > 0:
        entries = shard_levels(stream_key, shape, cuts, -0.22, 0.18) * entries
    return jnp.clip(entries, min=-most, max=most).astype(kind)


def setup_inputs(seed: int = 0) -> dict:
    splits = jax.random.split(jax.random.key(seed), 9)
    return {
        "tiles": normal_values(splits[0], (TILES, ROWS, D), 1.0, 6.0, ((0, 32), (2, 8))),
        "tile_counts": draw_tile_counts(jax.random.fold_in(splits[8], 71), 0),
        "encoder_rank": draw_encoder_rank(jax.random.fold_in(splits[8], 71), 0),
        "out_grad": normal_values(splits[3], (TILES, ROWS, D), 1.0, 6.0, ((0, 32), (2, 8))),
        "norm_gain": jnp.clip(jax.random.uniform(splits[4], (D,), jnp.float32, 0.5, 1.5), 0.5, 1.5),
        "layer_scale": jnp.clip(jax.random.uniform(splits[5], (D,), jnp.float32, 0.4, 1.6), 0.4, 1.6),
        "up_weight": normal_values(splits[6], (D, FF), D ** -0.5, 0.109375, ((1, 8),)),
        "down_weight": normal_values(splits[7], (D, FF), FF ** -0.5, 0.078125, ((1, 8),)),
    }


norm_eps = 1e-06
half_root = 0.7071067811865476
pdf_scale = 0.3989422804014327

def gelu_slope(values):
    return 0.5 * (1.0 + jax.scipy.special.erf(values * half_root)) + values * jnp.exp(-0.5 * values * values) * pdf_scale

def reference(tiles, tile_counts, encoder_rank, out_grad, norm_gain, layer_scale, up_weight, down_weight):
    slot_index = jnp.arange(SLOTS, dtype=jnp.int32)
    rank_ids = jnp.arange(N_DP, dtype=jnp.int32)
    counts = tile_counts.reshape(N_DP, SAMP_DEV)
    sample_hot = (slot_index // MAXT)[:, None] == jnp.arange(SAMP_DEV, dtype=jnp.int32)[None, :]
    per_slot = lax.optimization_barrier(jnp.sum(counts[:, None, :] * sample_hot[None, :, :].astype(jnp.int32), axis=2))
    is_live = (slot_index % MAXT)[None, :] < per_slot
    dest_table = encoder_rank.reshape(N_DP, SLOTS)
    hits = is_live[:, :, None] & (dest_table[:, :, None] == rank_ids[None, None, :])
    arrives = jnp.any(hits, axis=1).astype(jnp.int32)
    arrival_rank = jnp.cumsum(arrives, axis=0) - arrives
    position = jnp.take_along_axis(arrival_rank, dest_table.astype(jnp.int32), axis=1)
    target = jnp.where(is_live, dest_table * SLOTS + position, N_DP * SLOTS).reshape(-1).astype(jnp.int32)
    placed = jnp.zeros_like(tiles).at[target].set(tiles, mode='drop')
    received = lax.optimization_barrier(jnp.sum(arrives, axis=0))
    filled = (slot_index[None, :] < received[:, None]).reshape(-1)
    row_mask = jnp.repeat(filled, ROWS).astype(jnp.float32)[:, None]
    masked_grad = jnp.where(filled[:, None, None], out_grad, jnp.zeros_like(out_grad)).reshape(-1, D)
    x_rows = placed.reshape(-1, D)
    x_float = x_rows.astype(jnp.float32)
    radius = lax.rsqrt(lax.optimization_barrier(jnp.mean(x_float * x_float, axis=1, keepdims=True)) + norm_eps)
    normed = (x_float * radius * norm_gain).astype(jnp.bfloat16)
    pre_act = jnp.dot(normed, up_weight, preferred_element_type=jnp.float32)
    hidden = jax.nn.gelu(pre_act, approximate=False).astype(jnp.bfloat16)
    branch = lax.dot_general(hidden, down_weight, (((1,), (1,)), ((), ())), preferred_element_type=jnp.float32)
    embedded = ((x_float + layer_scale * branch) * row_mask).astype(jnp.bfloat16)
    grad_float = masked_grad.astype(jnp.float32)
    grad_out = (grad_float * layer_scale).astype(jnp.bfloat16)
    grad_hidden = jnp.dot(grad_out, down_weight, preferred_element_type=jnp.float32)
    grad_pre = (grad_hidden * gelu_slope(pre_act)).astype(jnp.bfloat16)
    grad_normed = lax.dot_general(grad_pre, up_weight, (((1,), (1,)), ((), ())), preferred_element_type=jnp.float32)
    scaled = grad_normed * norm_gain
    grad_input = radius * scaled - x_float * radius * radius * radius * lax.optimization_barrier(jnp.mean(scaled * x_float, axis=1, keepdims=True))
    tile_grads = ((grad_float + grad_input) * row_mask).astype(jnp.bfloat16)
    normed_ranks = normed.reshape(N_DP, SLOTS * ROWS, D)
    pre_ranks = grad_pre.reshape(N_DP, SLOTS * ROWS, FF)

    def add_rank(total, pieces):
        term = lax.dot_general(pieces[0], pieces[1], (((0,), (0,)), ((), ())), preferred_element_type=jnp.float32)
        return (total + term.astype(jnp.bfloat16).astype(jnp.float32), None)
    start = jnp.zeros((D, FF), jnp.float32)
    weight_sum, _ = lax.scan(add_rank, start, (normed_ranks, pre_ranks))
    weight_grads = weight_sum.astype(jnp.bfloat16)
    return (embedded.reshape(tiles.shape), tile_grads.reshape(tiles.shape), weight_grads)
```

```python
import functools

import jax
import jax.numpy as jnp
from jax import lax
from jax.experimental import pallas as pl
from jax.experimental.pallas import tpu as pltpu
from jax.sharding import PartitionSpec as P

norm_eps = 1e-06
half_root = 0.7071067811865476
pdf_scale = 0.3989422804014327
RING = 4
BF = jnp.bfloat16
F32 = jnp.float32


def round_up(value, to):
    return -(-value // to) * to


def make_sizes(mesh_dp, width, ff, slots, rows):
    s = {}
    s["NZ"] = mesh_dp // RING
    s["W"] = width
    s["F"] = ff
    s["SLOTS"] = slots
    s["R"] = rows
    s["T"] = slots * rows
    s["DP"] = mesh_dp
    s["FA"] = (ff // 2) // 128 * 128
    s["FB"] = ff - s["FA"]
    s["CB"] = s["NZ"] // 2
    s["CH"] = width // s["CB"]
    s["CP"] = round_up(s["CH"], 16)
    s["XW"] = width + 16
    s["LW"] = round_up(width + 16, 128)
    return s


def first_dims(left, right):
    return lax.dot_general(left, right, (((0,), (0,)), ((), ())), preferred_element_type=F32)


def last_dims(left, right):
    return lax.dot_general(left, right, (((1,), (1,)), ((), ())), preferred_element_type=F32)


def grid_of(shape, axis):
    return lax.broadcasted_iota(jnp.int32, shape, axis)


def kernel(
    s, n_copies,
    enc, cnt, tiles, out_grad, gain, scale, up_hbm, down_hbm,
    emb_out, tg_out, wg_out,
    up_v, down_v, out1, in1, out2, in2, g_all, x_all, wide, tall, placed_v, gm_v,
    hid_v, gpr_v, acc_v, gh_v, sel_v, px, xq, gpa, gpb,
    ps_o, pr_o, sb_o, rb_o, ps_g, pr_g, sb_g, rb_g,
    zsa, zra, zsb, zrb,
    wsem, send_sem, recv_sem,
):
    NZ, W, F, SLOTS, R, T, DP = (s[k] for k in ("NZ", "W", "F", "SLOTS", "R", "T", "DP"))
    FA, FB, CB, CH, CP, XW, LW = (s[k] for k in ("FA", "FB", "CB", "CH", "CP", "XW", "LW"))
    D = W * 2 * RING
    dp = lax.axis_index("dp")
    mp = lax.axis_index("mp")
    x, z = dp // NZ, dp % NZ
    y, c = mp // 2, mp % 2
    other = 1 - c

    def at_x(k):
        return {"dp": (x + k + RING) % RING * NZ + z, "mp": mp}

    def at_z(k):
        return {"dp": x * NZ + (z + k + NZ) % NZ, "mp": mp}

    def at_y(k):
        return {"dp": dp, "mp": (y + k + RING) % RING * 2 + c}

    partner = {"dp": dp, "mp": y * 2 + other}
    used = []

    def send(src, dst, device):
        at = len(used)
        copy = pltpu.make_async_remote_copy(
            src_ref=src, dst_ref=dst, send_sem=send_sem.at[at], recv_sem=recv_sem.at[at],
            device_id=device, device_id_type=pl.DeviceIdType.MESH,
        )
        copy.start()
        used.append(copy)
        return copy

    barrier = pltpu.get_barrier_semaphore()
    peers = [at_x(k) for k in range(1, RING)] + [at_z(k) for k in range(1, NZ)]
    peers += [at_y(1), at_y(-1), partner]
    for device in peers:
        pl.semaphore_signal(barrier, inc=1, device_id=device, device_id_type=pl.DeviceIdType.MESH)

    loads = []
    for j in range(2 * RING):
        loads.append(pltpu.make_async_copy(down_hbm.at[j], down_v.at[j], wsem.at[j]))
    for j in range(2 * RING):
        loads.append(pltpu.make_async_copy(up_hbm.at[j], up_v.at[j], wsem.at[2 * RING + j]))
    for load in loads:
        load.start()

    lane = grid_of((1, T), 1)
    dest = jnp.full((1, T), -1, jnp.int32)
    for j in range(SLOTS):
        live = (j % 8) < cnt[dp * (SLOTS // 8) + j // 8]
        goes = jnp.where(live, enc[dp * SLOTS + j], -1)
        dest = jnp.where((lane // R) == j, goes, dest)
    rows_all = DP * R
    row = grid_of((rows_all, T), 0)
    slot = row // R
    target = (slot % RING) * NZ + slot // RING
    picker = (target == dest) & ((row % R) == (grid_of((rows_all, T), 1) % R))
    picked = jnp.dot(picker.astype(BF), tiles[...], preferred_element_type=F32).astype(BF)
    out1[...] = picked.reshape(NZ, RING * R, W)

    pl.semaphore_wait(barrier, len(peers))
    stage1 = [send(out1.at[(z + k) % NZ], in1.at[z], at_z(k)) for k in range(1, NZ)]
    in1[z] = out1[z]

    lane_all = grid_of((1, rows_all), 1) // R

    def look(source, carry):
        count, order = carry
        comes = jnp.int32(0)
        for j in range(SLOTS):
            live = (j % 8) < cnt[source * (SLOTS // 8) + j // 8]
            here = enc[source * SLOTS + j] == dp
            comes = comes | (here.astype(jnp.int32) * live.astype(jnp.int32))
        order = jnp.where(
            lane_all == source, jnp.where(comes > 0, count, jnp.int32(SLOTS)), order
        )
        return count + comes, order

    count, order = lax.fori_loop(
        0, DP, look, (jnp.int32(0), jnp.full((1, rows_all), SLOTS, jnp.int32))
    )
    filled = (grid_of((T, 1), 0) // R) < count

    def local_part(ref):
        part = jnp.zeros((1, W), F32)
        for j in range(2 * RING):
            part = jnp.where(mp == j, ref[:, j * W : (j + 1) * W], part)
        return part

    gain_here = local_part(gain)
    scale_here = local_part(scale)

    masked = jnp.where(filled, out_grad[...].astype(F32), 0.0)
    gm_v[...] = masked
    wide[...] = jnp.zeros_like(wide)
    wide[:, :W] = masked * scale_here
    g_all[mp] = jnp.transpose(wide[...])[:W].astype(BF)

    def gather_1(buf):
        return (
            send(buf.at[mp], buf.at[mp], at_y(1)),
            send(buf.at[mp], buf.at[mp], at_y(-1)),
            send(buf.at[mp], buf.at[mp], partner),
        )

    from_left = (y + RING - 1) % RING * 2 + c
    from_right = (y + 1) % RING * 2 + c
    from_far = (y + 2) % RING * 2 + c

    def gather_2(buf, first, half, size):
        right, left, _ = first
        right.wait_recv()
        low = pl.ds(0, half)
        high = pl.ds(half, size - half)
        far_r = send(buf.at[from_left, low], buf.at[from_left, low], at_y(1))
        share_l = send(buf.at[from_left], buf.at[from_left], partner)
        left.wait_recv()
        far_l = send(buf.at[from_right, high], buf.at[from_right, high], at_y(-1))
        share_r = send(buf.at[from_right], buf.at[from_right], partner)
        return far_r, far_l, share_l, share_r

    def gather_3(buf, second, half, size):
        far_r, far_l, _, _ = second
        low = pl.ds(0, half)
        high = pl.ds(half, size - half)
        far_r.wait_recv()
        share_a = send(buf.at[from_far, low], buf.at[from_far, low], partner)
        far_l.wait_recv()
        share_b = send(buf.at[from_far, high], buf.at[from_far, high], partner)
        return share_a, share_b

    g_half = round_up(W // 2, 16)
    x_half = round_up(XW // 2, 16)
    g_first = gather_1(g_all)

    to_row = grid_of((rows_all, rows_all), 0)
    from_row = grid_of((rows_all, rows_all), 1)
    swap_slot = to_row // R
    wants = ((swap_slot % NZ) * RING + swap_slot // NZ) * R + to_row % R
    swap = (wants == from_row).astype(BF)
    for copy in stage1:
        copy.wait_recv()
    swapped = jnp.dot(
        swap, in1[...].reshape(rows_all, W), preferred_element_type=F32
    ).astype(BF)
    out2[...] = swapped.reshape(RING, NZ * R, W)
    stage2 = [send(out2.at[(x + k) % RING], in2.at[x], at_x(k)) for k in range(1, RING)]
    in2[x] = out2[x]

    g_second = gather_2(g_all, g_first, g_half, W)

    pack_row = grid_of((T, rows_all), 0)
    packer = ((pack_row // R) == order) & (
        (pack_row % R) == (grid_of((T, rows_all), 1) % R)
    )
    packer = packer.astype(BF)
    sel_row = grid_of((CB * CP, W), 0)
    sel_col = grid_of((CB * CP, W), 1)
    sel = jnp.zeros((CB * CP, W), jnp.bool_)
    for k in range(CB):
        sel = sel | (
            (sel_row - k * CP == sel_col - k * CH)
            & (sel_row >= k * CP)
            & (sel_row < k * CP + CH)
        )
    sel_v[...] = sel.astype(BF)

    for copy in stage2:
        copy.wait_recv()
    placed = jnp.dot(packer, in2[...].reshape(rows_all, W), preferred_element_type=F32)
    placed_v[...] = placed
    squares = jnp.sum(placed * placed, axis=1, keepdims=True)
    upper = squares.astype(BF).astype(F32)
    lower = squares - upper
    wide[:, :W] = placed * gain_here
    spread = wide[...]
    wide_lane = grid_of((T, LW), 1)
    spread = jnp.where(wide_lane == W, upper, jnp.where(wide_lane == W + 1, lower, spread))
    x_all[mp] = jnp.transpose(spread)[:XW].astype(BF)
    x_first = gather_1(x_all)

    g_third = gather_3(g_all, g_second, g_half, W)
    x_second = gather_2(x_all, x_first, x_half, XW)

    for copy in (g_first[2], g_second[2], g_second[3], g_third[0], g_third[1]):
        copy.wait_recv()
    for load in loads[: 2 * RING]:
        load.wait()
    gh_v[...] = jnp.zeros_like(gh_v)

    @pl.loop(0, 2 * RING)
    def _(j):
        gh_v[...] += first_dims(g_all[j], down_v[j])

    x_third = gather_3(x_all, x_second, x_half, XW)
    for load in loads[2 * RING :]:
        load.wait()
    for copy in (x_first[2], x_second[2], x_second[3], x_third[0], x_third[1]):
        copy.wait_recv()

    def quarter(block):
        moved = jnp.dot(sel_v[...], x_all[block, :W], preferred_element_type=F32)
        return moved.astype(BF).reshape(CB, CP, T)

    mine = pl.ds(c * CB, CB)
    xq_sent = []
    for at, k in enumerate((2, 1, 3)):
        px[at] = quarter((x + k) % RING * 2 + c)
        xq_sent.append(send(px.at[at], xq.at[x, mine], at_x(k)))
    acc_v[...] = jnp.zeros_like(acc_v)

    @pl.loop(0, 2 * RING)
    def _(j):
        acc_v[...] += first_dims(x_all[j, :W], up_v[j])

    tails = jnp.zeros((16, T), F32)
    for j in range(2 * RING):
        tails = tails + x_all[j, W:XW].astype(F32)
    total = jnp.sum(tails, axis=0, keepdims=True)
    radius = lax.rsqrt(
        jnp.transpose(jnp.broadcast_to(total, (128, T)))[:, :1] / D + norm_eps
    )

    def through(lo, hi):
        raw = acc_v[:, lo:hi]
        pre = radius * raw
        cdf = 0.5 * (1.0 + lax.erf(pre * half_root))
        slope = cdf + pre * jnp.exp(-0.5 * pre * pre) * pdf_scale
        hid_v[:, lo:hi] = (pre * cdf).astype(BF)
        back = (radius * (gh_v[:, lo:hi] * slope)).astype(BF)
        gpr_v[:, lo:hi] = back
        return back, jnp.sum(back.astype(F32) * raw, axis=1, keepdims=True)

    back_a, dot_a = through(0, FA)
    gpa[x] = back_a
    ga = (send(gpa.at[x], gpa.at[x], at_x(1)), send(gpa.at[x], gpa.at[x], at_x(-1)))
    back_b, dot_b = through(FA, F)
    gpb[x] = back_b
    gb = (send(gpb.at[x], gpb.at[x], at_x(1)), send(gpb.at[x], gpb.at[x], at_x(-1)))
    dots = jnp.transpose(jnp.broadcast_to((dot_a + dot_b) / D, (T, 128)))[:16]

    def block_of(k, core):
        return (y + k + RING) % RING * 2 + core

    def out_term(k, core):
        return last_dims(down_v[block_of(k, core)], hid_v[...])

    def grad_term(k, core):
        return last_dims(up_v[block_of(k, core)], gpr_v[...])

    steps = (2, 1, -1, 0)
    pair_o, pair_g = {}, {}
    for at, k in enumerate(steps):
        ps_o[at] = out_term(k, other).astype(BF)
        pair_o[k] = (at, send(ps_o.at[at], pr_o.at[at], partner))
    for at, k in enumerate((-2, 1, -1, 0)):
        ps_g[at, :W] = grad_term(k, other).astype(BF)
        ps_g[at, W:] = dots.astype(BF)
        pair_g[k] = (at, send(ps_g.at[at], pr_g.at[at], partner))

    def out_sum(k):
        at, copy = pair_o[k]
        term = out_term(k, c)
        copy.wait_recv()
        return term + pr_o[at].astype(F32)

    def grad_sum(k):
        at, copy = pair_g[k]
        term = grad_term(k, c)
        copy.wait_recv()
        both = pr_g[at].astype(F32)
        return term + both[:W], dots + both[W:]

    sb_o[0] = out_sum(2).astype(BF)
    o_far = send(sb_o.at[0], rb_o.at[0], at_y(1))
    main, tail = grad_sum(-2)
    sb_g[0, :W] = main.astype(BF)
    sb_g[0, W:] = tail.astype(BF)
    g_far = send(sb_g.at[0], rb_g.at[0], at_y(-1))
    sb_o[1] = out_sum(-1).astype(BF)
    o_left = send(sb_o.at[1], rb_o.at[1], at_y(-1))
    main, tail = grad_sum(1)
    sb_g[1, :W] = main.astype(BF)
    sb_g[1, W:] = tail.astype(BF)
    g_right = send(sb_g.at[1], rb_g.at[1], at_y(1))

    xq_shared = []
    for at, k in enumerate((2, 1, 3)):
        source = (x - k + RING) % RING
        xq_sent[at].wait_recv()
        xq_shared.append(send(xq.at[source, mine], xq.at[source, mine], partner))
    xl, xr = (x + RING - 1) % RING, (x + 1) % RING
    ga[0].wait_recv()
    ga_far = send(gpa.at[xl], gpa.at[xl], at_x(1))
    ga[1].wait_recv()
    gb[0].wait_recv()
    gb[1].wait_recv()
    gb_far = send(gpb.at[xr], gpb.at[xr], at_x(-1))
    for core in range(2):
        xq[x, core * CB : (core + 1) * CB] = quarter(x * 2 + core)

    main = out_sum(1)
    o_far.wait_recv()
    sb_o[2] = (main + rb_o[0].astype(F32)).astype(BF)
    o_right = send(sb_o.at[2], rb_o.at[2], at_y(1))
    main, tail = grad_sum(-1)
    g_far.wait_recv()
    sb_g[2, :W] = (main + rb_g[0, :W].astype(F32)).astype(BF)
    sb_g[2, W:] = (tail + rb_g[0, W:].astype(F32)).astype(BF)
    g_left = send(sb_g.at[2], rb_g.at[2], at_y(-1))

    for copy in xq_shared:
        copy.wait_recv()

    def weight_term(k, right):
        at = (z + k + NZ) % NZ
        left = jnp.concatenate([xq[r, at] for r in range(RING)], axis=1)
        return jnp.dot(left, right[...].reshape(RING * T, -1), preferred_element_type=F32)

    half = NZ // 2
    rings = []
    for right, sbuf, rbuf, up_dir in ((gpa, zsa, zra, 1), (gpb, zsb, zrb, -1)):
        rings.append((right, sbuf, rbuf, up_dir, half, []))
        rings.append((right, sbuf, rbuf, -up_dir, half - 1, []))

    def ring_step(ring, far, at):
        right, sbuf, rbuf, way, length, sent = ring
        step = len(sent)
        if step >= length:
            return
        d = length - step
        value = weight_term(way * d, right)
        if step > 0:
            sent[-1].wait_recv()
            value = value + rbuf[at - 1].astype(F32)
        sbuf[at] = value.astype(BF)
        sent.append(send(sbuf.at[at], rbuf.at[at], at_z(way)))

    def both_ways(pair, step):
        ring_step(rings[2 * pair], None, step)
        ring_step(rings[2 * pair + 1], None, half + step)

    ga_far.wait_recv()
    both_ways(0, 0)
    gb_far.wait_recv()
    both_ways(1, 0)

    main = out_sum(0)
    o_left.wait_recv()
    o_right.wait_recv()
    tall[...] = jnp.zeros_like(tall)
    tall[:W] = main + rb_o[1].astype(F32) + rb_o[2].astype(F32)
    branch = jnp.transpose(tall[...])[:, :W]
    emb_out[...] = jnp.where(filled, placed_v[...] + scale_here * branch, 0.0).astype(BF)

    both_ways(0, 1)
    both_ways(1, 1)

    main, tail = grad_sum(0)
    g_right.wait_recv()
    g_left.wait_recv()
    tall[:W] = main + rb_g[1, :W].astype(F32) + rb_g[2, :W].astype(F32)
    tall[W:XW] = tail + rb_g[1, W:].astype(F32) + rb_g[2, W:].astype(F32)
    turned = jnp.transpose(tall[...])
    mean_dot = turned[:, W : W + 1]
    grad_in = gain_here * turned[:, :W] - placed_v[...] * (radius * radius * mean_dot)
    tg_out[...] = jnp.where(filled, gm_v[...] + grad_in, 0.0).astype(BF)

    for step in range(2, half):
        both_ways(0, step)
        both_ways(1, step)

    for pair, lo, hi in ((0, 0, FA), (1, FA, F)):
        value = weight_term(0, rings[2 * pair][0])
        for which, base in ((0, 0), (1, half)):
            _, _, rbuf, _, length, sent = rings[2 * pair + which]
            if length > 0:
                sent[-1].wait_recv()
                value = value + rbuf[base + length - 1].astype(F32)
        wg_out[:, lo:hi] = value[:CH].astype(BF)

    for copy in used:
        copy.wait_send()
    assert len(used) <= n_copies, len(used)


def local(
    tiles, tile_counts, encoder_rank, out_grad, norm_gain, layer_scale, up_weight, down_weight
):
    slots, rows, width = tiles.shape
    ff = up_weight.shape[1]
    s = make_sizes(lax.axis_size("dp"), width, ff, slots, rows)
    NZ, W, F, T, DP = (s[k] for k in ("NZ", "W", "F", "T", "DP"))
    FA, FB, CB, CH, CP, XW, LW = (s[k] for k in ("FA", "FB", "CB", "CH", "CP", "XW", "LW"))
    D = W * 2 * RING
    n_copies = 60 + 6 * NZ
    vm = pl.BlockSpec(memory_space=pltpu.VMEM)
    sm = pl.BlockSpec(memory_space=pltpu.SMEM)
    hbm = pl.BlockSpec(memory_space=pl.ANY)
    scratch = [
        pltpu.VMEM((2 * RING, W, F), BF),
        pltpu.VMEM((2 * RING, W, F), BF),
        pltpu.VMEM((NZ, RING * rows, W), BF),
        pltpu.VMEM((NZ, RING * rows, W), BF),
        pltpu.VMEM((RING, NZ * rows, W), BF),
        pltpu.VMEM((RING, NZ * rows, W), BF),
        pltpu.VMEM((2 * RING, W, T), BF),
        pltpu.VMEM((2 * RING, XW, T), BF),
        pltpu.VMEM((T, LW), F32),
        pltpu.VMEM((LW, T), F32),
        pltpu.VMEM((T, W), F32),
        pltpu.VMEM((T, W), F32),
        pltpu.VMEM((T, F), BF),
        pltpu.VMEM((T, F), BF),
        pltpu.VMEM((T, F), F32),
        pltpu.VMEM((T, F), F32),
        pltpu.VMEM((CB * CP, W), BF),
        pltpu.VMEM((RING - 1, CB, CP, T), BF),
        pltpu.VMEM((RING, 2 * CB, CP, T), BF),
        pltpu.VMEM((RING, T, FA), BF),
        pltpu.VMEM((RING, T, FB), BF),
        pltpu.VMEM((4, W, T), BF),
        pltpu.VMEM((4, W, T), BF),
        pltpu.VMEM((3, W, T), BF),
        pltpu.VMEM((3, W, T), BF),
        pltpu.VMEM((4, XW, T), BF),
        pltpu.VMEM((4, XW, T), BF),
        pltpu.VMEM((3, XW, T), BF),
        pltpu.VMEM((3, XW, T), BF),
        pltpu.VMEM((NZ, CP, FA), BF),
        pltpu.VMEM((NZ, CP, FA), BF),
        pltpu.VMEM((NZ, CP, FB), BF),
        pltpu.VMEM((NZ, CP, FB), BF),
        pltpu.SemaphoreType.DMA((4 * RING,)),
        pltpu.SemaphoreType.DMA((n_copies,)),
        pltpu.SemaphoreType.DMA((n_copies,)),
    ]
    emb, tg, wg = pl.pallas_call(
        functools.partial(kernel, s, n_copies),
        out_shape=(
            jax.ShapeDtypeStruct((T, W), BF),
            jax.ShapeDtypeStruct((T, W), BF),
            jax.ShapeDtypeStruct((CH, F), BF),
        ),
        in_specs=[sm, sm, vm, vm, vm, vm, hbm, hbm],
        out_specs=(vm, vm, vm),
        scratch_shapes=scratch,
        compiler_params=pltpu.CompilerParams(
            collective_id=0, has_side_effects=True, vmem_limit_bytes=56 * 2**20
        ),
    )(
        encoder_rank,
        tile_counts,
        tiles.reshape(T, W),
        out_grad.reshape(T, W),
        norm_gain.reshape(1, D),
        layer_scale.reshape(1, D),
        up_weight.reshape(2 * RING, W, F),
        down_weight.reshape(2 * RING, W, F),
    )
    return emb.reshape(tiles.shape), tg.reshape(tiles.shape), wg


def solution(mesh):
    in_specs = (
        P("dp", None, "mp"),
        P(),
        P(),
        P("dp", None, "mp"),
        P(),
        P(),
        P(None, "mp"),
        P(None, "mp"),
    )
    out_specs = (P("dp", None, "mp"), P("dp", None, "mp"), P("dp", "mp"))
    return jax.shard_map(local, mesh=mesh, in_specs=in_specs, out_specs=out_specs, check_vma=False)
```

```python
import functools

import jax
import jax.numpy as jnp
from jax import lax
from jax.experimental import pallas as pl
from jax.experimental.pallas import tpu as pltpu
from jax.sharding import PartitionSpec as P

norm_eps = 1e-06
half_root = 0.7071067811865476
pdf_scale = 0.3989422804014327
RING = 4
BF = jnp.bfloat16
F32 = jnp.float32


def round_up(value, to):
    return -(-value // to) * to


def make_sizes(mesh_dp, width, ff, slots, rows):
    s = {}
    s["NZ"] = mesh_dp // RING
    s["W"] = width
    s["F"] = ff
    s["SLOTS"] = slots
    s["R"] = rows
    s["T"] = slots * rows
    s["DP"] = mesh_dp
    s["FA"] = (ff // 2) // 128 * 128
    s["FB"] = ff - s["FA"]
    s["CB"] = s["NZ"] // 2
    s["CH"] = width // s["CB"]
    s["CP"] = round_up(s["CH"], 16)
    s["XW"] = width + 16
    s["LW"] = round_up(width + 16, 128)
    return s


def first_dims(left, right):
    return lax.dot_general(left, right, (((0,), (0,)), ((), ())), preferred_element_type=F32)


def last_dims(left, right):
    return lax.dot_general(left, right, (((1,), (1,)), ((), ())), preferred_element_type=F32)


def grid_of(shape, axis):
    return lax.broadcasted_iota(jnp.int32, shape, axis)


def kernel(
    s, n_copies,
    enc, cnt, tiles_hbm, grad_hbm, gain, scale, up_hbm, down_hbm,
    emb_out, tg_out, wg_out,
    up_v, down_v, tiles, out_grad, emb_v, tg_v, wg_v,
    out1, in1, out2, in2, g_all, x_all, sq_pair, sq_ring, wide, tall, placed_v, gm_v,
    hid_v, gpr_v, acc_v, gh_v, out_t, grad_t, sel_v, px, xq, gpa, gpb,
    ps_o, pr_o, sb_o, rb_o, ps_g, pr_g, sb_g, rb_g,
    zsa, zra, zsb, zrb,
    wsem, osem, send_sem, recv_sem,
):
    NZ, W, F, SLOTS, R, T, DP = (s[k] for k in ("NZ", "W", "F", "SLOTS", "R", "T", "DP"))
    FA, FB, CB, CH, CP, XW, LW = (s[k] for k in ("FA", "FB", "CB", "CH", "CP", "XW", "LW"))
    D = W * 2 * RING
    dp = lax.axis_index("dp")
    mp = lax.axis_index("mp")
    x, z = dp // NZ, dp % NZ
    y, c = mp // 2, mp % 2
    other = 1 - c

    def at_x(k):
        return {"dp": (x + k + RING) % RING * NZ + z, "mp": mp}

    def at_z(k):
        return {"dp": x * NZ + (z + k + NZ) % NZ, "mp": mp}

    def at_y(k):
        return {"dp": dp, "mp": (y + k + RING) % RING * 2 + c}

    partner = {"dp": dp, "mp": y * 2 + other}
    used = []

    def send(src, dst, device):
        at = len(used)
        copy = pltpu.make_async_remote_copy(
            src_ref=src, dst_ref=dst, send_sem=send_sem.at[at], recv_sem=recv_sem.at[at],
            device_id=device, device_id_type=pl.DeviceIdType.MESH,
        )
        copy.start()
        used.append(copy)
        return copy

    barrier = pltpu.get_barrier_semaphore()
    peers = [at_x(k) for k in range(1, RING)] + [at_z(k) for k in range(1, NZ)]
    peers += [at_y(1), at_y(2), at_y(3), partner]
    for device in peers:
        pl.semaphore_signal(barrier, inc=1, device_id=device, device_id_type=pl.DeviceIdType.MESH)

    first = pltpu.make_async_copy(tiles_hbm, tiles, wsem.at[0])
    first.start()
    second = pltpu.make_async_copy(grad_hbm, out_grad, wsem.at[1])
    second.start()
    load_down = pltpu.make_async_copy(down_hbm, down_v, wsem.at[2])
    load_down.start()
    load_up = pltpu.make_async_copy(up_hbm, up_v, wsem.at[3])
    load_up.start()

    def block(j):
        return pl.ds(pl.multiple_of(j * W, 16), W)

    def part(j, lo, size):
        return pl.ds(pl.multiple_of(j * W + lo, 16), size)

    lane = grid_of((1, T), 1)
    dest = jnp.full((1, T), -1, jnp.int32)
    for j in range(SLOTS):
        live = (j % 8) < cnt[dp * (SLOTS // 8) + j // 8]
        goes = jnp.where(live, enc[dp * SLOTS + j], -1)
        dest = jnp.where((lane // R) == j, goes, dest)
    rows_all = DP * R
    row = grid_of((rows_all, T), 0)
    slot = row // R
    target = (slot % RING) * NZ + slot // RING
    picker = (target == dest) & ((row % R) == (grid_of((rows_all, T), 1) % R))
    first.wait()
    picked = jnp.dot(picker.astype(BF), tiles[...], preferred_element_type=F32).astype(BF)
    out1[...] = picked.reshape(NZ, RING * R, W)

    pl.semaphore_wait(barrier, len(peers))
    stage1 = [send(out1.at[(z + k) % NZ], in1.at[z], at_z(k)) for k in range(1, NZ)]
    in1[z] = out1[z]

    lane_all = grid_of((1, rows_all), 1) // R

    def look(source, carry):
        count, order = carry
        comes = jnp.int32(0)
        for j in range(SLOTS):
            live = (j % 8) < cnt[source * (SLOTS // 8) + j // 8]
            here = enc[source * SLOTS + j] == dp
            comes = comes | (here.astype(jnp.int32) * live.astype(jnp.int32))
        order = jnp.where(
            lane_all == source, jnp.where(comes > 0, count, jnp.int32(SLOTS)), order
        )
        return count + comes, order

    count, order = lax.fori_loop(
        0, DP, look, (jnp.int32(0), jnp.full((1, rows_all), SLOTS, jnp.int32))
    )
    filled = (grid_of((T, 1), 0) // R) < count

    def local_part(ref):
        whole = ref[...].reshape(1, D)
        part = jnp.zeros((1, W), F32)
        for j in range(2 * RING):
            part = jnp.where(mp == j, whole[:, j * W : (j + 1) * W], part)
        return part

    gain_here = local_part(gain)
    scale_here = local_part(scale)

    second.wait()
    masked = jnp.where(filled, out_grad[...].astype(F32), 0.0)
    gm_v[...] = masked
    wide[...] = jnp.zeros_like(wide)
    wide[:, :W] = masked * scale_here
    g_all[block(mp)] = jnp.transpose(wide[...])[:W].astype(BF)

    def gather_1(buf):
        own = buf.at[block(mp)]
        return send(own, own, at_y(1)), send(own, own, at_y(-1)), send(own, own, partner)

    from_left = (y + RING - 1) % RING * 2 + c
    from_right = (y + 1) % RING * 2 + c
    from_far = (y + 2) % RING * 2 + c
    low = round_up(W // 2, 16)

    def gather_2(buf, first):
        right, left, _ = first
        right.wait_recv()
        piece = buf.at[part(from_left, 0, low)]
        far_r = send(piece, piece, at_y(1))
        piece = buf.at[block(from_left)]
        share_l = send(piece, piece, partner)
        left.wait_recv()
        piece = buf.at[part(from_right, low, W - low)]
        far_l = send(piece, piece, at_y(-1))
        piece = buf.at[block(from_right)]
        share_r = send(piece, piece, partner)
        return far_r, far_l, share_l, share_r

    def gather_3(buf, second):
        far_r, far_l, _, _ = second
        far_r.wait_recv()
        piece = buf.at[part(from_far, 0, low)]
        share_a = send(piece, piece, partner)
        far_l.wait_recv()
        piece = buf.at[part(from_far, low, W - low)]
        share_b = send(piece, piece, partner)
        return share_a, share_b

    g_first = gather_1(g_all)

    to_row = grid_of((rows_all, rows_all), 0)
    from_row = grid_of((rows_all, rows_all), 1)
    swap_slot = to_row // R
    wants = ((swap_slot % NZ) * RING + swap_slot // NZ) * R + to_row % R
    swap = (wants == from_row).astype(BF)
    for copy in stage1:
        copy.wait_recv()
    swapped = jnp.dot(
        swap, in1[...].reshape(rows_all, W), preferred_element_type=F32
    ).astype(BF)
    out2[...] = swapped.reshape(RING, NZ * R, W)
    stage2 = [send(out2.at[(x + k) % RING], in2.at[x], at_x(k)) for k in range(1, RING)]
    in2[x] = out2[x]

    g_second = gather_2(g_all, g_first)

    pack_row = grid_of((T, rows_all), 0)
    packer = ((pack_row // R) == order) & (
        (pack_row % R) == (grid_of((T, rows_all), 1) % R)
    )
    packer = packer.astype(BF)
    sel_row = grid_of((CB * CP, W), 0)
    sel_col = grid_of((CB * CP, W), 1)
    sel = jnp.zeros((CB * CP, W), jnp.bool_)
    for k in range(CB):
        sel = sel | (
            (sel_row - k * CP == sel_col - k * CH)
            & (sel_row >= k * CP)
            & (sel_row < k * CP + CH)
        )
    sel_v[...] = sel.astype(BF)

    for copy in stage2:
        copy.wait_recv()
    placed = jnp.dot(packer, in2[...].reshape(rows_all, W), preferred_element_type=F32)
    placed_v[...] = placed
    wide[:, :W] = placed * gain_here
    x_all[block(mp)] = jnp.transpose(wide[...])[:W].astype(BF)
    x_first = gather_1(x_all)
    wide[:, :W] = placed * placed
    squares = jnp.sum(jnp.transpose(wide[...]), axis=0, keepdims=True)
    sq_pair[0] = jnp.broadcast_to(squares, (8, T))
    sq_sent = send(sq_pair.at[0], sq_pair.at[1], partner)

    g_third = gather_3(g_all, g_second)
    sq_sent.wait_recv()
    sq_ring[0] = sq_pair[0] + sq_pair[1]
    sq_parts = [send(sq_ring.at[0], sq_ring.at[k], at_y(k)) for k in range(1, RING)]
    x_second = gather_2(x_all, x_first)

    for copy in (g_first[2], g_second[2], g_second[3], g_third[0], g_third[1]):
        copy.wait_recv()
    load_down.wait()
    gh_v[...] = jnp.dot(down_v[...], g_all[...], preferred_element_type=F32)

    x_third = gather_3(x_all, x_second)
    load_up.wait()
    for copy in (x_first[2], x_second[2], x_second[3], x_third[0], x_third[1]):
        copy.wait_recv()

    def quarter(j):
        moved = jnp.dot(sel_v[...], x_all[block(j)], preferred_element_type=F32)
        return moved.astype(BF).reshape(CB, CP, T)

    mine = pl.ds(c * CB, CB)
    xq_sent = []
    for at, k in enumerate((2, 1, 3)):
        px[at] = quarter((x + k) % RING * 2 + c)
        xq_sent.append(send(px.at[at], xq.at[x, mine], at_x(k)))
    acc_v[...] = jnp.dot(up_v[...], x_all[...], preferred_element_type=F32)

    for copy in sq_parts:
        copy.wait_recv()
    total = sq_ring[0] + sq_ring[1] + sq_ring[2] + sq_ring[3]
    radius = lax.rsqrt(total[:1] / D + norm_eps)

    def through(lo, hi):
        raw = acc_v[lo:hi]
        pre = radius * raw
        cdf = 0.5 * (1.0 + lax.erf(pre * half_root))
        slope = cdf + pre * jnp.exp(-0.5 * pre * pre) * pdf_scale
        acc_v[lo:hi] = pre * cdf
        back = radius * (gh_v[lo:hi] * slope)
        gh_v[lo:hi] = back
        return back.astype(BF), jnp.sum(back * raw, axis=0, keepdims=True)

    back_a, dot_a = through(0, FA)
    gpa[x] = back_a
    ga = (send(gpa.at[x], gpa.at[x], at_x(1)), send(gpa.at[x], gpa.at[x], at_x(-1)))
    back_b, dot_b = through(FA, F)
    gpb[x] = back_b
    gb = (send(gpb.at[x], gpb.at[x], at_x(1)), send(gpb.at[x], gpb.at[x], at_x(-1)))
    dots = jnp.broadcast_to((dot_a + dot_b) / D, (16, T))

    def turn_rows(ref):
        whole = ref[: F // 128 * 128]
        parts = [jnp.transpose(whole)]
        if F % 128:
            last = jnp.concatenate([ref[F // 128 * 128 :], jnp.zeros((128 - F % 128, T), F32)], axis=0)
            parts.append(jnp.transpose(last))
        return jnp.concatenate(parts, axis=1)[:, :F].astype(BF)

    tile = D // 5 if D % 640 == 0 else 128

    hid_v[...] = turn_rows(acc_v)

    @pl.loop(0, D // tile)
    def _(t):
        cols = pl.ds(pl.multiple_of(t * tile, 128), tile)
        some = jnp.dot(hid_v[...], down_v[:, cols], preferred_element_type=F32)
        out_t[cols] = jnp.transpose(some)

    gpr_v[...] = turn_rows(gh_v)

    @pl.loop(0, D // tile)
    def _(t):
        cols = pl.ds(pl.multiple_of(t * tile, 128), tile)
        some = jnp.dot(gpr_v[...], up_v[:, cols], preferred_element_type=F32)
        grad_t[cols] = jnp.transpose(some)

    def block_of(k, core):
        return (y + k + RING) % RING * 2 + core

    def out_term(k, core):
        return out_t[block(block_of(k, core))]

    def grad_term(k, core):
        return grad_t[block(block_of(k, core))]

    steps = (2, 1, -1, 0)
    pair_o, pair_g = {}, {}
    for at, k in enumerate(steps):
        ps_o[at] = out_term(k, other).astype(BF)
        pair_o[k] = (at, send(ps_o.at[at], pr_o.at[at], partner))
    for at, k in enumerate((-2, 1, -1, 0)):
        ps_g[at, :W] = grad_term(k, other).astype(BF)
        ps_g[at, W:] = dots.astype(BF)
        pair_g[k] = (at, send(ps_g.at[at], pr_g.at[at], partner))

    def out_sum(k):
        at, copy = pair_o[k]
        term = out_term(k, c)
        copy.wait_recv()
        return term + pr_o[at].astype(F32)

    def grad_sum(k):
        at, copy = pair_g[k]
        term = grad_term(k, c)
        copy.wait_recv()
        both = pr_g[at].astype(F32)
        return term + both[:W], dots + both[W:]

    sb_o[0] = out_sum(2).astype(BF)
    o_far = send(sb_o.at[0], rb_o.at[0], at_y(1))
    main, tail = grad_sum(-2)
    sb_g[0, :W] = main.astype(BF)
    sb_g[0, W:] = tail.astype(BF)
    g_far = send(sb_g.at[0], rb_g.at[0], at_y(-1))
    sb_o[1] = out_sum(-1).astype(BF)
    o_left = send(sb_o.at[1], rb_o.at[1], at_y(-1))
    main, tail = grad_sum(1)
    sb_g[1, :W] = main.astype(BF)
    sb_g[1, W:] = tail.astype(BF)
    g_right = send(sb_g.at[1], rb_g.at[1], at_y(1))

    xq_shared = []
    for at, k in enumerate((2, 1, 3)):
        source = (x - k + RING) % RING
        xq_sent[at].wait_recv()
        xq_shared.append(send(xq.at[source, mine], xq.at[source, mine], partner))
    xl, xr = (x + RING - 1) % RING, (x + 1) % RING
    ga[0].wait_recv()
    ga_far = send(gpa.at[xl], gpa.at[xl], at_x(1))
    ga[1].wait_recv()
    gb[0].wait_recv()
    gb[1].wait_recv()
    gb_far = send(gpb.at[xr], gpb.at[xr], at_x(-1))
    for core in range(2):
        xq[x, core * CB : (core + 1) * CB] = quarter(x * 2 + core)

    main = out_sum(1)
    o_far.wait_recv()
    sb_o[2] = (main + rb_o[0].astype(F32)).astype(BF)
    o_right = send(sb_o.at[2], rb_o.at[2], at_y(1))
    main, tail = grad_sum(-1)
    g_far.wait_recv()
    sb_g[2, :W] = (main + rb_g[0, :W].astype(F32)).astype(BF)
    sb_g[2, W:] = (tail + rb_g[0, W:].astype(F32)).astype(BF)
    g_left = send(sb_g.at[2], rb_g.at[2], at_y(-1))

    for copy in xq_shared:
        copy.wait_recv()

    def weight_term(k, right):
        at = (z + k + NZ) % NZ
        left = jnp.concatenate([xq[r, at] for r in range(RING)], axis=1)
        turned = jnp.concatenate([right[r] for r in range(RING)], axis=1)
        return last_dims(left, turned)

    half = NZ // 2
    rings = []
    for right, sbuf, rbuf, up_dir in ((gpa, zsa, zra, 1), (gpb, zsb, zrb, -1)):
        rings.append((right, sbuf, rbuf, up_dir, half, []))
        rings.append((right, sbuf, rbuf, -up_dir, half - 1, []))

    def ring_step(ring, far, at):
        right, sbuf, rbuf, way, length, sent = ring
        step = len(sent)
        if step >= length:
            return
        d = length - step
        value = weight_term(way * d, right)
        if step > 0:
            sent[-1].wait_recv()
            value = value + rbuf[at - 1].astype(F32)
        sbuf[at] = value.astype(BF)
        sent.append(send(sbuf.at[at], rbuf.at[at], at_z(way)))

    def both_ways(pair, step):
        ring_step(rings[2 * pair], None, step)
        ring_step(rings[2 * pair + 1], None, half + step)

    ga_far.wait_recv()
    both_ways(0, 0)
    gb_far.wait_recv()
    both_ways(1, 0)

    main = out_sum(0)
    o_left.wait_recv()
    o_right.wait_recv()
    tall[...] = jnp.zeros_like(tall)
    tall[:W] = main + rb_o[1].astype(F32) + rb_o[2].astype(F32)
    branch = jnp.transpose(tall[...])[:, :W]
    emb_v[...] = jnp.where(filled, placed_v[...] + scale_here * branch, 0.0).astype(BF)
    store_emb = pltpu.make_async_copy(emb_v, emb_out, osem.at[0])
    store_emb.start()

    both_ways(0, 1)
    both_ways(1, 1)

    main, tail = grad_sum(0)
    g_right.wait_recv()
    g_left.wait_recv()
    tall[:W] = main + rb_g[1, :W].astype(F32) + rb_g[2, :W].astype(F32)
    tail = tail + rb_g[1, W:].astype(F32) + rb_g[2, W:].astype(F32)
    tall[W:XW] = tail * (radius * radius)
    turned = jnp.transpose(tall[...])
    mean_dot = turned[:, W : W + 1]
    grad_in = gain_here * turned[:, :W] - placed_v[...] * mean_dot
    tg_v[...] = jnp.where(filled, gm_v[...] + grad_in, 0.0).astype(BF)
    store_tg = pltpu.make_async_copy(tg_v, tg_out, osem.at[1])
    store_tg.start()

    for step in range(2, half):
        both_ways(0, step)
        both_ways(1, step)

    for pair, lo, hi in ((0, 0, FA), (1, FA, F)):
        value = weight_term(0, rings[2 * pair][0])
        for which, base in ((0, 0), (1, half)):
            _, _, rbuf, _, length, sent = rings[2 * pair + which]
            if length > 0:
                sent[-1].wait_recv()
                value = value + rbuf[base + length - 1].astype(F32)
        wg_v[:, lo:hi] = value[:CH].astype(BF)
    store_wg = pltpu.make_async_copy(wg_v, wg_out, osem.at[2])
    store_wg.start()

    for copy in used:
        copy.wait_send()
    store_emb.wait()
    store_tg.wait()
    store_wg.wait()
    assert len(used) <= n_copies, len(used)


def hand_over_kernel(a, b, c, a_out, b_out, c_out, sem):
    copies = [
        pltpu.make_async_copy(src, dst, sem.at[at])
        for at, (src, dst) in enumerate(((a, a_out), (b, b_out), (c, c_out)))
    ]
    for copy in copies:
        copy.start()
    for copy in copies:
        copy.wait()


def hand_over(*arrays):
    hbm = pl.BlockSpec(memory_space=pl.ANY)
    return pl.pallas_call(
        hand_over_kernel,
        out_shape=tuple(jax.ShapeDtypeStruct(a.shape, a.dtype) for a in arrays),
        in_specs=[hbm] * 3,
        out_specs=(hbm,) * 3,
        scratch_shapes=[pltpu.SemaphoreType.DMA((3,))],
    )(*arrays)


def local(
    tiles, tile_counts, encoder_rank, out_grad, norm_gain, layer_scale, up_weight, down_weight
):
    slots, rows, width = tiles.shape
    ff = up_weight.shape[1]
    s = make_sizes(lax.axis_size("dp"), width, ff, slots, rows)
    NZ, W, F, T, DP = (s[k] for k in ("NZ", "W", "F", "T", "DP"))
    FA, FB, CB, CH, CP, XW, LW = (s[k] for k in ("FA", "FB", "CB", "CH", "CP", "XW", "LW"))
    D = W * 2 * RING
    n_copies = 60 + 6 * NZ
    vm = pl.BlockSpec(memory_space=pltpu.VMEM)
    sm = pl.BlockSpec(memory_space=pltpu.SMEM)
    hbm = pl.BlockSpec(memory_space=pl.ANY)
    scratch = [
        pltpu.VMEM((F, D), BF),
        pltpu.VMEM((F, D), BF),
        pltpu.VMEM((T, W), BF),
        pltpu.VMEM((T, W), BF),
        pltpu.VMEM((T, W), BF),
        pltpu.VMEM((T, W), BF),
        pltpu.VMEM((CH, F), BF),
        pltpu.VMEM((NZ, RING * rows, W), BF),
        pltpu.VMEM((NZ, RING * rows, W), BF),
        pltpu.VMEM((RING, NZ * rows, W), BF),
        pltpu.VMEM((RING, NZ * rows, W), BF),
        pltpu.VMEM((D, T), BF),
        pltpu.VMEM((D, T), BF),
        pltpu.VMEM((2, 8, T), F32),
        pltpu.VMEM((RING, 8, T), F32),
        pltpu.VMEM((T, LW), F32),
        pltpu.VMEM((LW, T), F32),
        pltpu.VMEM((T, W), F32),
        pltpu.VMEM((T, W), F32),
        pltpu.VMEM((T, F), BF),
        pltpu.VMEM((T, F), BF),
        pltpu.VMEM((F, T), F32),
        pltpu.VMEM((F, T), F32),
        pltpu.VMEM((D, T), F32),
        pltpu.VMEM((D, T), F32),
        pltpu.VMEM((CB * CP, W), BF),
        pltpu.VMEM((RING - 1, CB, CP, T), BF),
        pltpu.VMEM((RING, 2 * CB, CP, T), BF),
        pltpu.VMEM((RING, FA, T), BF),
        pltpu.VMEM((RING, FB, T), BF),
        pltpu.VMEM((4, W, T), BF),
        pltpu.VMEM((4, W, T), BF),
        pltpu.VMEM((3, W, T), BF),
        pltpu.VMEM((3, W, T), BF),
        pltpu.VMEM((4, XW, T), BF),
        pltpu.VMEM((4, XW, T), BF),
        pltpu.VMEM((3, XW, T), BF),
        pltpu.VMEM((3, XW, T), BF),
        pltpu.VMEM((NZ, CP, FA), BF),
        pltpu.VMEM((NZ, CP, FA), BF),
        pltpu.VMEM((NZ, CP, FB), BF),
        pltpu.VMEM((NZ, CP, FB), BF),
        pltpu.SemaphoreType.DMA((4,)),
        pltpu.SemaphoreType.DMA((3,)),
        pltpu.SemaphoreType.DMA((n_copies,)),
        pltpu.SemaphoreType.DMA((n_copies,)),
    ]
    emb, tg, wg = pl.pallas_call(
        functools.partial(kernel, s, n_copies),
        out_shape=(
            jax.ShapeDtypeStruct((T, W), BF),
            jax.ShapeDtypeStruct((T, W), BF),
            jax.ShapeDtypeStruct((CH, F), BF),
        ),
        in_specs=[sm, sm, hbm, hbm, vm, vm, hbm, hbm],
        out_specs=(hbm, hbm, hbm),
        scratch_shapes=scratch,
        compiler_params=pltpu.CompilerParams(
            collective_id=0, has_side_effects=True, vmem_limit_bytes=56 * 2**20
        ),
    )(
        encoder_rank,
        tile_counts,
        tiles.reshape(T, W),
        out_grad.reshape(T, W),
        norm_gain,
        layer_scale,
        up_weight.T,
        down_weight.T,
    )
    emb, tg, wg = hand_over(emb, tg, wg)
    return emb.reshape(tiles.shape), tg.reshape(tiles.shape), wg


def solution(mesh):
    in_specs = (
        P("dp", None, "mp"),
        P(),
        P(),
        P("dp", None, "mp"),
        P(),
        P(),
        P(None, "mp"),
        P(None, "mp"),
    )
    out_specs = (P("dp", None, "mp"), P("dp", None, "mp"), P("dp", "mp"))
    return jax.shard_map(local, mesh=mesh, in_specs=in_specs, out_specs=out_specs, check_vma=False)
```

```python
import functools

import jax
import jax.numpy as jnp
from jax import lax
from jax.experimental import pallas as pl
from jax.experimental.pallas import tpu as pltpu
from jax.sharding import PartitionSpec as P

norm_eps = 1e-06
half_root = 0.7071067811865476
pdf_scale = 0.3989422804014327
RING = 4
BF = jnp.bfloat16
F32 = jnp.float32


def round_up(value, to):
    return -(-value // to) * to


def make_sizes(mesh_dp, width, ff, slots, rows):
    s = {}
    s["NZ"] = mesh_dp // RING
    s["W"] = width
    s["F"] = ff
    s["SLOTS"] = slots
    s["R"] = rows
    s["T"] = slots * rows
    s["DP"] = mesh_dp
    s["FP"] = ff // 3 // 128 * 128
    s["FL"] = ff - 3 * s["FP"]
    s["CB"] = s["NZ"] // 2
    s["CH"] = width // s["CB"]
    s["CP"] = round_up(s["CH"], 8)
    s["XW"] = width + 16
    s["LW"] = round_up(width + 16, 128)
    return s


def first_dims(left, right):
    return lax.dot_general(left, right, (((0,), (0,)), ((), ())), preferred_element_type=F32)


def last_dims(left, right):
    return lax.dot_general(left, right, (((1,), (1,)), ((), ())), preferred_element_type=F32)


def grid_of(shape, axis):
    return lax.broadcasted_iota(jnp.int32, shape, axis)


def kernel(
    s, n_copies,
    enc, cnt, tiles_hbm, grad_hbm, gain, scale, up_hbm, down_hbm,
    emb_out, tg_out, wg_out,
    up_v, down_v, tiles, out_grad, emb_v, tg_v, wg_v,
    out1, in1, g_all, x_all, sq_pair, sq_ring, wide, tall, placed_v, gm_v,
    hid_v, gpr_v, gh_v, out_t, grad_t, sel_v, px, xq, gp0, gp1, gp2,
    ps_o, pr_o, sb_o, rb_o, ps_g, pr_g, sb_g, rb_g,
    zs0, zr0, zs1, zr1, zs2, zr2, zs3, zr3,
    wsem, osem, send_sem, recv_sem,
):
    NZ, W, F, SLOTS, R, T, DP = (s[k] for k in ("NZ", "W", "F", "SLOTS", "R", "T", "DP"))
    FP, FL, CB, CH, CP, XW, LW = (s[k] for k in ("FP", "FL", "CB", "CH", "CP", "XW", "LW"))
    D = W * 2 * RING
    dp = lax.axis_index("dp")
    mp = lax.axis_index("mp")
    x, z = dp // NZ, dp % NZ
    y, c = mp // 2, mp % 2
    other = 1 - c

    def at_x(k):
        return {"dp": (x + k + RING) % RING * NZ + z, "mp": mp}

    def at_z(k):
        return {"dp": x * NZ + (z + k + NZ) % NZ, "mp": mp}

    def at_xz(i, k):
        return {"dp": (x + i) % RING * NZ + (z + k) % NZ, "mp": mp}

    def at_y(k):
        return {"dp": dp, "mp": (y + k + RING) % RING * 2 + c}

    partner = {"dp": dp, "mp": y * 2 + other}
    used = []

    def send(src, dst, device):
        at = len(used)
        copy = pltpu.make_async_remote_copy(
            src_ref=src, dst_ref=dst, send_sem=send_sem.at[at], recv_sem=recv_sem.at[at],
            device_id=device, device_id_type=pl.DeviceIdType.MESH,
        )
        copy.start()
        used.append(copy)
        return copy

    barrier = pltpu.get_barrier_semaphore()
    others = [(i, k) for k in range(NZ) for i in range(RING) if (i, k) != (0, 0)]
    others.sort(key=lambda ik: -min(ik[0], RING - ik[0]) - min(ik[1], NZ - ik[1]))
    peers = [at_xz(i, k) for i, k in others]
    peers += [at_y(1), at_y(2), at_y(3), partner]
    for device in peers:
        pl.semaphore_signal(barrier, inc=1, device_id=device, device_id_type=pl.DeviceIdType.MESH)

    first = pltpu.make_async_copy(tiles_hbm, tiles, wsem.at[0])
    first.start()
    second = pltpu.make_async_copy(grad_hbm, out_grad, wsem.at[1])
    second.start()
    load_down = pltpu.make_async_copy(down_hbm, down_v, wsem.at[2])
    load_down.start()
    load_up = pltpu.make_async_copy(up_hbm, up_v, wsem.at[3])
    load_up.start()

    def block(j):
        return pl.ds(pl.multiple_of(j * W, 16), W)

    def part(j, lo, size):
        return pl.ds(pl.multiple_of(j * W + lo, 16), size)

    lane = grid_of((1, T), 1)
    dest = jnp.full((1, T), -1, jnp.int32)
    for j in range(SLOTS):
        live = (j % 8) < cnt[dp * (SLOTS // 8) + j // 8]
        goes = jnp.where(live, enc[dp * SLOTS + j], -1)
        dest = jnp.where((lane // R) == j, goes, dest)
    rows_all = DP * R
    row = grid_of((rows_all, T), 0)
    picker = ((row // R) == dest) & ((row % R) == (grid_of((rows_all, T), 1) % R))
    first.wait()
    picked = jnp.dot(picker.astype(BF), tiles[...], preferred_element_type=F32)
    out1[...] = picked.reshape(DP, R, W).astype(BF)

    pl.semaphore_wait(barrier, len(peers))
    exchange = []
    for i, k in others:
        there = (x + i) % RING * NZ + (z + k) % NZ
        exchange.append(send(out1.at[there], in1.at[dp], at_xz(i, k)))
    in1[dp] = out1[dp]

    lane_all = grid_of((1, rows_all), 1) // R

    def look(source, carry):
        count, order = carry
        comes = jnp.int32(0)
        for j in range(SLOTS):
            live = (j % 8) < cnt[source * (SLOTS // 8) + j // 8]
            here = enc[source * SLOTS + j] == dp
            comes = comes | (here.astype(jnp.int32) * live.astype(jnp.int32))
        order = jnp.where(
            lane_all == source, jnp.where(comes > 0, count, jnp.int32(SLOTS)), order
        )
        return count + comes, order

    count, order = lax.fori_loop(
        0, DP, look, (jnp.int32(0), jnp.full((1, rows_all), SLOTS, jnp.int32))
    )
    filled = (grid_of((T, 1), 0) // R) < count

    def local_part(ref):
        whole = ref[...].reshape(1, D)
        part = jnp.zeros((1, W), F32)
        for j in range(2 * RING):
            part = jnp.where(mp == j, whole[:, j * W : (j + 1) * W], part)
        return part

    gain_here = local_part(gain)
    scale_here = local_part(scale)

    second.wait()
    masked = jnp.where(filled, out_grad[...].astype(F32), 0.0)
    gm_v[...] = masked
    wide[...] = jnp.zeros_like(wide)
    wide[:, :W] = masked * scale_here
    g_all[block(mp)] = jnp.transpose(wide[...])[:W].astype(BF)

    ways = (2, 1, 3)

    def gather_1(buf):
        own = buf.at[block(mp)]
        return [send(own, own, partner)] + [send(own, own, at_y(k)) for k in ways]

    def gather_2(buf, copy, k):
        copy.wait_recv()
        piece = buf.at[block((y - k + RING) % RING * 2 + c)]
        return send(piece, piece, partner)

    g_first = gather_1(g_all)

    pack_row = grid_of((T, rows_all), 0)
    packer = ((pack_row // R) == order) & (
        (pack_row % R) == (grid_of((T, rows_all), 1) % R)
    )
    packer = packer.astype(BF)
    sel_row = grid_of((CB * CP, W), 0)
    sel_col = grid_of((CB * CP, W), 1)
    sel = jnp.zeros((CB * CP, W), jnp.bool_)
    for k in range(CB):
        sel = sel | (
            (sel_row - k * CP == sel_col - k * CH)
            & (sel_row >= k * CP)
            & (sel_row < k * CP + CH)
        )
    sel_v[...] = sel.astype(BF)

    for copy in exchange:
        copy.wait_recv()
    arrived = in1[...].astype(F32).reshape(rows_all, W).astype(BF)
    placed = jnp.dot(packer, arrived, preferred_element_type=F32)
    placed_v[...] = placed
    wide[:, :W] = placed * gain_here
    x_all[block(mp)] = jnp.transpose(wide[...])[:W].astype(BF)
    x_first = gather_1(x_all)
    wide[:, :W] = placed * placed
    squares = jnp.sum(jnp.transpose(wide[...]), axis=0, keepdims=True)
    sq_pair[0] = jnp.broadcast_to(squares, (8, T))
    sq_sent = send(sq_pair.at[0], sq_pair.at[1], partner)

    mine = pl.ds(c * CB, CB)
    theirs = pl.ds(other * CB, CB)

    def quarter(j):
        moved = jnp.dot(sel_v[...], x_all[block(j)], preferred_element_type=F32)
        return moved.reshape(CB, CP, T).astype(BF)

    g_second = [gather_2(g_all, copy, k) for copy, k in zip(g_first[1:], ways)]
    for copy in [g_first[0]] + g_second:
        copy.wait_recv()
    load_down.wait()
    gh_v[...] = jnp.dot(down_v[...], g_all[...], preferred_element_type=F32)
    sq_sent.wait_recv()
    sq_ring[0] = sq_pair[0] + sq_pair[1]
    sq_parts = [send(sq_ring.at[0], sq_ring.at[k], at_y(k)) for k in range(1, RING)]

    x_second = []
    for at, k in ((2, 1), (3, 3), (1, 2)):
        x_second.append(gather_2(x_all, x_first[at], k))
    load_up.wait()
    for copy in [x_first[0]] + x_second:
        copy.wait_recv()
    xq_sent = {}
    for way in ways:
        px[way] = quarter((x + way) % RING * 2 + c)
        xq_sent[way] = send(px.at[way], xq.at[x, mine], at_x(way))

    for copy in sq_parts:
        copy.wait_recv()
    total = sq_ring[0] + sq_ring[1] + sq_ring[2] + sq_ring[3]
    radius = lax.rsqrt(total[:1] / D + norm_eps)

    def through(buf, lo, hi):
        raw = jnp.dot(up_v[lo:hi], x_all[...], preferred_element_type=F32)
        pre = radius * raw
        cdf = 0.5 * (1.0 + lax.erf(pre * half_root))
        slope = cdf + pre * jnp.exp(-0.5 * pre * pre) * pdf_scale
        hid_v[lo:hi] = (pre * cdf).astype(BF)
        back = radius * (gh_v[lo:hi] * slope)
        short = back.astype(BF)
        buf[x] = short
        gpr_v[lo:hi] = short
        sent = [send(buf.at[x], buf.at[x], at_x(k)) for k in (2, 1, 3)]
        return sent, jnp.sum(back * raw, axis=0, keepdims=True)

    gp_sent = []
    dots = jnp.zeros((1, T), F32)
    for buf, lo, hi in ((gp0, 0, FP), (gp1, FP, 2 * FP), (gp2, 2 * FP, F)):
        sent, dot = through(buf, lo, hi)
        gp_sent.append(sent)
        dots = dots + dot
    dots = jnp.broadcast_to(dots / D, (16, T))
    xq[x, mine] = quarter(x * 2 + c)
    xq[x, theirs] = quarter(x * 2 + other)

    out_t[...] = first_dims(down_v[...], hid_v[...])

    def block_of(k, core):
        return (y + k + RING) % RING * 2 + core

    def out_term(k, core):
        return out_t[block(block_of(k, core))]

    def grad_term(k, core):
        return grad_t[block(block_of(k, core))]

    pair_o, pair_g = {}, {}
    for at, k in enumerate((2, 1, 3, 0)):
        ps_o[at] = out_term(k, other).astype(BF)
        pair_o[k] = (at, send(ps_o.at[at], pr_o.at[at], partner))

    xq_shared = []
    for way in (1, 3, 2):
        source = (x - way + RING) % RING
        xq_sent[way].wait_recv()
        xq_shared.append(send(xq.at[source, mine], xq.at[source, mine], partner))

    grad_t[...] = first_dims(up_v[...], gpr_v[...])
    for at, k in enumerate((2, 1, 3, 0)):
        ps_g[at, :W] = grad_term(k, other).astype(BF)
        ps_g[at, W:] = dots.astype(BF)
        pair_g[k] = (at, send(ps_g.at[at], pr_g.at[at], partner))

    def out_sum(k):
        at, copy = pair_o[k]
        term = out_term(k, c)
        copy.wait_recv()
        return term + pr_o[at].astype(F32)

    def grad_sum(k):
        at, copy = pair_g[k]
        term = grad_term(k, c)
        copy.wait_recv()
        both = pr_g[at].astype(F32)
        return term + both[:W], dots + both[W:]

    for copy in xq_shared:
        copy.wait_recv()

    def left_rows(k):
        at = (z + k + NZ) % NZ
        return jnp.concatenate([xq[r, at] for r in range(RING)], axis=1)

    def turned(buf, lo, hi):
        return jnp.concatenate([buf[r, lo:hi] for r in range(RING)], axis=1)

    def term_of(buf):
        return lambda k: last_dims(left_rows(k), turned(buf, 0, FP))

    per = 128 // FL
    high = round_up(-(-CP // per), 16)
    lane_group = grid_of((high, 128), 1) // FL

    def rest_term(k):
        rest = turned(gp2, FP, FP + FL)
        wide_rest = last_dims(left_rows(k), jnp.concatenate([rest] * per, axis=0))
        folded = jnp.zeros((high, 128), F32)
        for g in range(per):
            rows = wide_rest[g * high : (g + 1) * high]
            if rows.shape[0] < high:
                pad = jnp.zeros((high - rows.shape[0], 128), F32)
                rows = jnp.concatenate([rows, pad], axis=0)
            folded = jnp.where(lane_group == g, rows, folded)
        return folded

    half = NZ // 2
    plan = (
        (term_of(gp0), zs0, zr0, 1),
        (term_of(gp1), zs1, zr1, -1),
        (term_of(gp2), zs2, zr2, 1),
        (rest_term, zs3, zr3, -1),
    )
    rings = []
    for term, sbuf, rbuf, way in plan:
        rings.append(((term, sbuf, rbuf, way, half, 0), []))
        rings.append(((term, sbuf, rbuf, -way, half - 1, half), []))

    def ring_step(ring, step):
        (term, sbuf, rbuf, way, length, base), sent = ring
        if step >= length:
            return
        at = base + step
        value = term(way * (length - step))
        if step > 0:
            sent[-1].wait_recv()
            value = value + rbuf[at - 1].astype(F32)
        sbuf[at] = value.astype(BF)
        sent.append(send(sbuf.at[at], rbuf.at[at], at_z(way)))

    def both_ways(piece, step):
        ring_step(rings[2 * piece], step)
        ring_step(rings[2 * piece + 1], step)

    for copy in gp_sent[0]:
        copy.wait_recv()
    both_ways(0, 0)
    o_sent = []
    for at, k in enumerate(ways):
        sb_o[at] = out_sum(k).astype(BF)
        o_sent.append(send(sb_o.at[at], rb_o.at[at], at_y(k)))
    for copy in gp_sent[1]:
        copy.wait_recv()
    both_ways(1, 0)
    g_sent = []
    for at, k in enumerate(ways):
        main, tail = grad_sum(k)
        sb_g[at, :W] = main.astype(BF)
        sb_g[at, W:] = tail.astype(BF)
        g_sent.append(send(sb_g.at[at], rb_g.at[at], at_y(k)))
    both_ways(0, 1)
    for copy in gp_sent[2]:
        copy.wait_recv()
    both_ways(2, 0)
    both_ways(3, 0)
    both_ways(1, 1)

    main = out_sum(0)
    for at, copy in enumerate(o_sent):
        copy.wait_recv()
        main = main + rb_o[at].astype(F32)
    tall[...] = jnp.zeros_like(tall)
    tall[:W] = main
    branch = jnp.transpose(tall[...])[:, :W]
    emb_v[...] = jnp.where(filled, placed_v[...] + scale_here * branch, 0.0).astype(BF)
    store_emb = pltpu.make_async_copy(emb_v, emb_out, osem.at[0])
    store_emb.start()

    both_ways(0, 2)
    both_ways(2, 1)
    both_ways(3, 1)
    both_ways(1, 2)

    main, tail = grad_sum(0)
    for at, copy in enumerate(g_sent):
        copy.wait_recv()
        main = main + rb_g[at, :W].astype(F32)
        tail = tail + rb_g[at, W:].astype(F32)
    tall[:W] = main
    tall[W:XW] = tail * (radius * radius)
    upright = jnp.transpose(tall[...])
    mean_dot = upright[:, W : W + 1]
    grad_in = gain_here * upright[:, :W] - placed_v[...] * mean_dot
    tg_v[...] = jnp.where(filled, gm_v[...] + grad_in, 0.0).astype(BF)
    store_tg = pltpu.make_async_copy(tg_v, tg_out, osem.at[1])
    store_tg.start()

    both_ways(0, 3)
    both_ways(2, 2)
    both_ways(3, 2)
    both_ways(1, 3)

    def ring_end(piece):
        value = rings[2 * piece][0][0](0)
        for (_, _, rbuf, _, length, base), sent in rings[2 * piece : 2 * piece + 2]:
            sent[-1].wait_recv()
            value = value + rbuf[base + length - 1].astype(F32)
        return value

    wg_v[:, :FP] = ring_end(0)[:CH].astype(BF)
    both_ways(2, 3)
    both_ways(3, 3)
    wg_v[:, FP : 2 * FP] = ring_end(1)[:CH].astype(BF)
    wg_v[:, 2 * FP : 3 * FP] = ring_end(2)[:CH].astype(BF)
    folded = ring_end(3)
    unfolded = [folded[:, g * FL : (g + 1) * FL] for g in range(per)]
    wg_v[:, 3 * FP :] = jnp.concatenate(unfolded, axis=0)[:CH].astype(BF)
    store_wg = pltpu.make_async_copy(wg_v, wg_out, osem.at[2])
    store_wg.start()

    for copy in used:
        copy.wait_send()
    store_emb.wait()
    store_tg.wait()
    store_wg.wait()
    assert len(used) <= n_copies, len(used)


def hand_over_kernel(a, b, c, a_out, b_out, c_out, a_v, b_v, c_v, sem):
    arrays = ((a, a_v, a_out), (b, b_v, b_out), (c, c_v, c_out))
    loads = [pltpu.make_async_copy(src, mid, sem.at[i]) for i, (src, mid, _) in enumerate(arrays)]
    stores = [pltpu.make_async_copy(mid, dst, sem.at[3 + i]) for i, (_, mid, dst) in enumerate(arrays)]
    for load in loads:
        load.start()
    for load, store in zip(loads, stores):
        load.wait()
        store.start()
    for store in stores:
        store.wait()


def hand_over(*arrays):
    hbm = pl.BlockSpec(memory_space=pl.ANY)
    return pl.pallas_call(
        hand_over_kernel,
        out_shape=tuple(jax.ShapeDtypeStruct(a.shape, a.dtype) for a in arrays),
        in_specs=[hbm] * 3,
        out_specs=(hbm,) * 3,
        scratch_shapes=[pltpu.VMEM(a.shape, a.dtype) for a in arrays]
        + [pltpu.SemaphoreType.DMA((6,))],
    )(*arrays)


def local(
    tiles, tile_counts, encoder_rank, out_grad, norm_gain, layer_scale, up_weight, down_weight
):
    slots, rows, width = tiles.shape
    ff = up_weight.shape[1]
    s = make_sizes(lax.axis_size("dp"), width, ff, slots, rows)
    NZ, W, F, T, DP = (s[k] for k in ("NZ", "W", "F", "T", "DP"))
    FP, FL, CB, CH, CP, XW, LW = (s[k] for k in ("FP", "FL", "CB", "CH", "CP", "XW", "LW"))
    D = W * 2 * RING
    n_copies = 160
    folded = (round_up(-(-CP // (128 // FL)), 16), 128)
    vm = pl.BlockSpec(memory_space=pltpu.VMEM)
    sm = pl.BlockSpec(memory_space=pltpu.SMEM)
    hbm = pl.BlockSpec(memory_space=pl.ANY)
    scratch = [
        pltpu.VMEM((F, D), BF),
        pltpu.VMEM((F, D), BF),
        pltpu.VMEM((T, W), BF),
        pltpu.VMEM((T, W), BF),
        pltpu.VMEM((T, W), BF),
        pltpu.VMEM((T, W), BF),
        pltpu.VMEM((CH, F), BF),
        pltpu.VMEM((DP, rows, W), BF),
        pltpu.VMEM((DP, rows, W), BF),
        pltpu.VMEM((D, T), BF),
        pltpu.VMEM((D, T), BF),
        pltpu.VMEM((2, 8, T), F32),
        pltpu.VMEM((RING, 8, T), F32),
        pltpu.VMEM((T, LW), F32),
        pltpu.VMEM((LW, T), F32),
        pltpu.VMEM((T, W), F32),
        pltpu.VMEM((T, W), F32),
        pltpu.VMEM((F, T), BF),
        pltpu.VMEM((F, T), BF),
        pltpu.VMEM((F, T), F32),
        pltpu.VMEM((D, T), F32),
        pltpu.VMEM((D, T), F32),
        pltpu.VMEM((CB * CP, W), BF),
        pltpu.VMEM((RING, CB, CP, T), BF),
        pltpu.VMEM((RING, 2 * CB, CP, T), BF),
        pltpu.VMEM((RING, FP, T), BF),
        pltpu.VMEM((RING, FP, T), BF),
        pltpu.VMEM((RING, FP + FL, T), BF),
        pltpu.VMEM((4, W, T), BF),
        pltpu.VMEM((4, W, T), BF),
        pltpu.VMEM((3, W, T), BF),
        pltpu.VMEM((3, W, T), BF),
        pltpu.VMEM((4, XW, T), BF),
        pltpu.VMEM((4, XW, T), BF),
        pltpu.VMEM((3, XW, T), BF),
        pltpu.VMEM((3, XW, T), BF),
    ]
    for _ in range(6):
        scratch.append(pltpu.VMEM((NZ, CP, FP), BF))
    for _ in range(2):
        scratch.append(pltpu.VMEM((NZ,) + folded, BF))
    scratch += [
        pltpu.SemaphoreType.DMA((4,)),
        pltpu.SemaphoreType.DMA((3,)),
        pltpu.SemaphoreType.DMA((n_copies,)),
        pltpu.SemaphoreType.DMA((n_copies,)),
    ]
    emb, tg, wg = pl.pallas_call(
        functools.partial(kernel, s, n_copies),
        out_shape=(
            jax.ShapeDtypeStruct((T, W), BF),
            jax.ShapeDtypeStruct((T, W), BF),
            jax.ShapeDtypeStruct((CH, F), BF),
        ),
        in_specs=[sm, sm, hbm, hbm, vm, vm, hbm, hbm],
        out_specs=(hbm, hbm, hbm),
        scratch_shapes=scratch,
        compiler_params=pltpu.CompilerParams(
            collective_id=0, has_side_effects=True, vmem_limit_bytes=56 * 2**20
        ),
    )(
        encoder_rank,
        tile_counts,
        tiles.reshape(T, W),
        out_grad.reshape(T, W),
        norm_gain,
        layer_scale,
        up_weight.T,
        down_weight.T,
    )
    emb, tg, wg = hand_over(emb, tg, wg)
    return emb.reshape(tiles.shape), tg.reshape(tiles.shape), wg


def solution(mesh):
    in_specs = (
        P("dp", None, "mp"),
        P(),
        P(),
        P("dp", None, "mp"),
        P(),
        P(),
        P(None, "mp"),
        P(None, "mp"),
    )
    out_specs = (P("dp", None, "mp"), P("dp", None, "mp"), P("dp", "mp"))
    return jax.shard_map(local, mesh=mesh, in_specs=in_specs, out_specs=out_specs, check_vma=False)
```

```python
import functools

import jax
import jax.numpy as jnp
from jax import lax
from jax.experimental import pallas as pl
from jax.experimental.pallas import tpu as pltpu
from jax.sharding import PartitionSpec as P

norm_eps = 1e-06
half_root = 0.7071067811865476
pdf_scale = 0.3989422804014327
RING = 4
BF = jnp.bfloat16
F32 = jnp.float32


def round_up(value, to):
    return -(-value // to) * to


def make_sizes(mesh_dp, width, ff, slots, rows):
    s = {}
    s["NZ"] = mesh_dp // RING
    s["W"] = width
    s["F"] = ff
    s["SLOTS"] = slots
    s["R"] = rows
    s["T"] = slots * rows
    s["DP"] = mesh_dp
    s["FP"] = ff // 3 // 128 * 128
    s["FL"] = ff - 3 * s["FP"]
    s["CB"] = s["NZ"] // 2
    s["CH"] = width // s["CB"]
    s["CP"] = round_up(s["CH"], 8)
    s["XW"] = width + 16
    s["LW"] = round_up(width + 16, 128)
    return s


def first_dims(left, right):
    return lax.dot_general(left, right, (((0,), (0,)), ((), ())), preferred_element_type=F32)


def last_dims(left, right):
    return lax.dot_general(left, right, (((1,), (1,)), ((), ())), preferred_element_type=F32)


def grid_of(shape, axis):
    return lax.broadcasted_iota(jnp.int32, shape, axis)


def kernel(
    s, n_copies,
    enc_hbm, cnt_hbm, tiles_hbm, grad_hbm, gain_hbm, scale_hbm, up_hbm, down_hbm,
    emb_out, tg_out, wg_out,
    enc, cnt, gain, scale, up_v, down_v, tiles, out_grad, emb_v, tg_v, wg_v,
    out1, in1, g_all, x_all, sq_pair, sq_ring, wide, tall, placed_v, gm_v,
    hid_v, gpr_v, gh_v, out_t, grad_t, sel_v, px, xq, gp0, gp1, gp2,
    ps_o, pr_o, sb_o, rb_o, ps_g, pr_g, sb_g, rb_g,
    zs0, zr0, zs1, zr1, zs2, zr2, zs3, zr3,
    wsem, osem, sems,
):
    NZ, W, F, SLOTS, R, T, DP = (s[k] for k in ("NZ", "W", "F", "SLOTS", "R", "T", "DP"))
    FP, FL, CB, CH, CP, XW, LW = (s[k] for k in ("FP", "FL", "CB", "CH", "CP", "XW", "LW"))
    D = W * 2 * RING
    dp = lax.axis_index("dp")
    mp = lax.axis_index("mp")
    x, z = dp // NZ, dp % NZ
    y, c = mp // 2, mp % 2
    other = 1 - c

    def at_x(k):
        return {"dp": (x + k + RING) % RING * NZ + z, "mp": mp}

    def at_z(k):
        return {"dp": x * NZ + (z + k + NZ) % NZ, "mp": mp}

    def at_xz(i, k):
        return {"dp": (x + i) % RING * NZ + (z + k) % NZ, "mp": mp}

    def at_y(k):
        return {"dp": dp, "mp": (y + k + RING) % RING * 2 + c}

    partner = {"dp": dp, "mp": y * 2 + other}
    taken = []
    sent_later = []

    def new():
        taken.append(len(taken))
        return taken[-1]

    def send(src, dst, device, sent, got):
        copy = pltpu.make_async_remote_copy(
            src_ref=src, dst_ref=dst, send_sem=sems.at[sent], recv_sem=sems.at[got],
            device_id=device, device_id_type=pl.DeviceIdType.MESH,
        )
        copy.start()

    def wait(at, like):
        pltpu.make_async_copy(like, like, sems.at[at]).wait()

    def outgoing(like):
        at = new()
        sent_later.append((at, like))
        return at

    smalls = []
    for at, (src, dst) in enumerate(
        ((enc_hbm, enc), (cnt_hbm, cnt), (gain_hbm, gain), (scale_hbm, scale))
    ):
        smalls.append(pltpu.make_async_copy(src, dst, wsem.at[4 + at]))
    first = pltpu.make_async_copy(tiles_hbm, tiles, wsem.at[0])
    second = pltpu.make_async_copy(grad_hbm, out_grad, wsem.at[1])
    for small in smalls[:2] + [first] + smalls[2:] + [second]:
        small.start()

    barrier = pltpu.get_barrier_semaphore()
    others = [(i, k) for k in range(NZ) for i in range(RING) if (i, k) != (0, 0)]
    others.sort(key=lambda ik: -min(ik[0], RING - ik[0]) - min(ik[1], NZ - ik[1]))
    peers = [at_xz(i, k) for i, k in others]
    peers += [at_y(1), at_y(2), at_y(3), partner]
    for device in peers:
        pl.semaphore_signal(barrier, inc=1, device_id=device, device_id_type=pl.DeviceIdType.MESH)

    load_down = pltpu.make_async_copy(down_hbm, down_v, wsem.at[2])
    load_down.start()
    load_up = pltpu.make_async_copy(up_hbm, up_v, wsem.at[3])
    load_up.start()

    def block(j):
        return pl.ds(pl.multiple_of(j * W, 16), W)

    def part(j, lo, size):
        return pl.ds(pl.multiple_of(j * W + lo, 16), size)

    lane = grid_of((1, T), 1)
    smalls[0].wait()
    smalls[1].wait()
    dest = jnp.full((1, T), -1, jnp.int32)
    for j in range(SLOTS):
        live = (j % 8) < cnt[dp * (SLOTS // 8) + j // 8]
        goes = jnp.where(live, enc[dp * SLOTS + j], -1)
        dest = jnp.where((lane // R) == j, goes, dest)
    rows_all = DP * R
    row = grid_of((rows_all, T), 0)
    picker = ((row // R) == dest) & ((row % R) == (grid_of((rows_all, T), 1) % R))
    first.wait()
    picked = jnp.dot(picker.astype(BF), tiles[...], preferred_element_type=F32)
    out1[...] = picked.reshape(DP, R, W).astype(BF)

    pl.semaphore_wait(barrier, len(peers))
    ex_out, ex_in = outgoing(out1.at[pl.ds(0, DP - 1)]), new()
    for i, k in others:
        there = (x + i) % RING * NZ + (z + k) % NZ
        send(out1.at[there], in1.at[dp], at_xz(i, k), ex_out, ex_in)
    in1[dp] = out1[dp]

    lane_all = grid_of((1, rows_all), 1) // R

    def look(source, carry):
        count, order = carry
        comes = jnp.int32(0)
        for j in range(SLOTS):
            live = (j % 8) < cnt[source * (SLOTS // 8) + j // 8]
            here = enc[source * SLOTS + j] == dp
            comes = comes | (here.astype(jnp.int32) * live.astype(jnp.int32))
        order = jnp.where(
            lane_all == source, jnp.where(comes > 0, count, jnp.int32(SLOTS)), order
        )
        return count + comes, order

    count, order = lax.fori_loop(
        0, DP, look, (jnp.int32(0), jnp.full((1, rows_all), SLOTS, jnp.int32))
    )
    filled = (grid_of((T, 1), 0) // R) < count

    def local_part(ref):
        whole = ref[...].reshape(1, D)
        part = jnp.zeros((1, W), F32)
        for j in range(2 * RING):
            part = jnp.where(mp == j, whole[:, j * W : (j + 1) * W], part)
        return part

    smalls[2].wait()
    smalls[3].wait()
    gain_here = local_part(gain)
    scale_here = local_part(scale)

    second.wait()
    masked = jnp.where(filled, out_grad[...].astype(F32), 0.0)
    gm_v[...] = masked
    wide[...] = jnp.zeros_like(wide)
    wide[:, :W] = masked * scale_here
    g_all[block(mp)] = jnp.transpose(wide[...])[:W].astype(BF)

    ways = (2, 1, 3)

    seven = pl.ds(0, 7 * W)
    four = pl.ds(0, 4 * W)
    three = pl.ds(0, 3 * W)
    one = pl.ds(0, W)
    inner = pl.ds(1, RING - 1)

    def gather_1(buf, sent, pair, along):
        own = buf.at[block(mp)]
        send(own, own, partner, sent, pair)
        for k in ways:
            send(own, own, at_y(k), sent, along[k])

    def gather_2(buf, k, sent, pair):
        piece = buf.at[block((y - k + RING) % RING * 2 + c)]
        send(piece, piece, partner, sent, pair)

    g_out, g_pair, g_along = outgoing(g_all.at[seven]), new(), new()
    gather_1(g_all, g_out, g_pair, {k: g_along for k in ways})

    pack_row = grid_of((T, rows_all), 0)
    packer = ((pack_row // R) == order) & (
        (pack_row % R) == (grid_of((T, rows_all), 1) % R)
    )
    packer = packer.astype(BF)
    sel_row = grid_of((CB * CP, W), 0)
    sel_col = grid_of((CB * CP, W), 1)
    sel = jnp.zeros((CB * CP, W), jnp.bool_)
    for k in range(CB):
        sel = sel | (
            (sel_row - k * CP == sel_col - k * CH)
            & (sel_row >= k * CP)
            & (sel_row < k * CP + CH)
        )
    sel_v[...] = sel.astype(BF)
    sel_row = grid_of((CP, W), 0)
    sel_y = ((sel_row + y * CH) == grid_of((CP, W), 1)) & (sel_row < CH)
    sel_y = sel_y.astype(BF)

    wait(ex_in, in1.at[pl.ds(0, DP - 1)])
    arrived = in1[...].astype(F32).reshape(rows_all, W).astype(BF)
    placed = jnp.dot(packer, arrived, preferred_element_type=F32)
    placed_v[...] = placed
    wide[:, :W] = placed * gain_here
    x_all[block(mp)] = jnp.transpose(wide[...])[:W].astype(BF)
    x_out, x_pair = outgoing(x_all.at[seven]), new()
    x_along = {k: new() for k in ways}
    gather_1(x_all, x_out, x_pair, x_along)
    wide[:, :W] = placed * placed
    squares = jnp.sum(jnp.transpose(wide[...]), axis=0, keepdims=True)
    sq_pair[0] = jnp.broadcast_to(squares, (8, T))
    sq_got = new()
    send(sq_pair.at[0], sq_pair.at[1], partner, outgoing(sq_pair.at[0]), sq_got)

    mine = pl.ds(c * CB, CB)
    theirs = pl.ds(other * CB, CB)

    def quarter(j):
        moved = jnp.dot(sel_v[...], x_all[block(j)], preferred_element_type=F32)
        return moved.reshape(CB, CP, T).astype(BF)

    wait(g_along, g_all.at[three])
    for k in ways:
        gather_2(g_all, k, g_out, g_pair)
    wait(g_pair, g_all.at[four])
    load_down.wait()
    gh_v[...] = jnp.dot(down_v[...], g_all[...], preferred_element_type=F32)
    wait(sq_got, sq_pair.at[0])
    sq_ring[0] = sq_pair[0] + sq_pair[1]
    sq_out, sq_in = outgoing(sq_ring.at[inner]), new()
    for k in ways:
        send(sq_ring.at[0], sq_ring.at[k], at_y(k), sq_out, sq_in)

    for k in ways:
        wait(x_along[k], x_all.at[one])
        gather_2(x_all, k, x_out, x_pair)
    load_up.wait()
    wait(x_pair, x_all.at[four])
    part_y = c * CB + y
    xq_out, xq_in = outgoing(px), new()
    for way in ways:
        piece = x_all[block((x + way) % RING * 2 + c)]
        px[way - 1] = jnp.dot(sel_y, piece, preferred_element_type=F32).astype(BF)
        send(px.at[way - 1], xq.at[way, part_y], at_x(way), xq_out, xq_in)
    wait(sq_in, sq_ring.at[inner])
    total = sq_ring[0] + sq_ring[1] + sq_ring[2] + sq_ring[3]
    radius = lax.rsqrt(total[:1] / D + norm_eps)

    def through(buf, lo, hi):
        raw = jnp.dot(up_v[lo:hi], x_all[...], preferred_element_type=F32)
        pre = radius * raw
        cdf = 0.5 * (1.0 + lax.erf(pre * half_root))
        slope = cdf + pre * jnp.exp(-0.5 * pre * pre) * pdf_scale
        hid_v[lo:hi] = (pre * cdf).astype(BF)
        back = radius * (gh_v[lo:hi] * slope)
        short = back.astype(BF)
        buf[0] = short
        gpr_v[lo:hi] = short
        sent, got = outgoing(buf.at[inner]), new()
        for k in ways:
            send(buf.at[0], buf.at[k], at_x(k), sent, got)
        return got, jnp.sum(back * raw, axis=0, keepdims=True)

    gp_in = []
    dots = jnp.zeros((1, T), F32)
    for buf, lo, hi in ((gp0, 0, FP + FL), (gp1, FP + FL, 2 * FP + FL), (gp2, 2 * FP + FL, F)):
        got, dot = through(buf, lo, hi)
        gp_in.append(got)
        dots = dots + dot
    dots = jnp.broadcast_to(dots / D, (16, T))
    wait(xq_in, px)
    xq_y_out, xq_y_in = outgoing(xq.at[inner, inner]), new()
    for k in ways:
        piece = xq.at[inner, part_y]
        send(piece, piece, at_y(k), xq_y_out, xq_y_in)
    xq[0, mine] = quarter(x * 2 + c)
    xq[0, theirs] = quarter(x * 2 + other)

    out_t[...] = first_dims(down_v[...], hid_v[...])

    def block_of(k, core):
        return (y + k + RING) % RING * 2 + core

    def out_term(k, core):
        return out_t[block(block_of(k, core))]

    def grad_term(k, core):
        return grad_t[block(block_of(k, core))]

    order = (2, 1, 3, 0)
    po_out, po_in = outgoing(ps_o), new()
    for at, k in enumerate(order):
        ps_o[at] = out_term(k, other).astype(BF)
        send(ps_o.at[at], pr_o.at[at], partner, po_out, po_in)

    grad_t[...] = first_dims(up_v[...], gpr_v[...])
    pg_out, pg_in = outgoing(ps_g), new()
    for at, k in enumerate(order):
        ps_g[at, :W] = grad_term(k, other).astype(BF)
        ps_g[at, W:] = dots.astype(BF)
        send(ps_g.at[at], pr_g.at[at], partner, pg_out, pg_in)

    def out_sum(at):
        return out_term(order[at], c) + pr_o[at].astype(F32)

    def grad_sum(at):
        both = pr_g[at].astype(F32)
        return grad_term(order[at], c) + both[:W], dots + both[W:]

    wait(po_in, pr_o)
    so_out, so_in = outgoing(sb_o), new()
    for at, k in enumerate(ways):
        sb_o[at] = out_sum(at).astype(BF)
        send(sb_o.at[at], rb_o.at[at], at_y(k), so_out, so_in)

    wait(xq_y_in, xq.at[inner, inner])
    xq_p_in = new()
    piece = xq.at[inner, mine]
    send(piece, piece, partner, outgoing(piece), xq_p_in)
    wait(xq_p_in, xq.at[inner, theirs])

    def left_rows(k):
        at = (z + k + NZ) % NZ
        return jnp.concatenate([xq[r, at] for r in range(RING)], axis=1)

    def turned(buf, lo, hi):
        return jnp.concatenate([buf[r, lo:hi] for r in range(RING)], axis=1)

    def term_of(buf):
        return lambda k: last_dims(left_rows(k), turned(buf, 0, FP))

    per = 128 // FL
    high = round_up(-(-CP // per), 16)
    lane_group = grid_of((high, 128), 1) // FL

    def rest_term(k):
        rest = turned(gp0, FP, FP + FL)
        wide_rest = last_dims(left_rows(k), jnp.concatenate([rest] * per, axis=0))
        folded = jnp.zeros((high, 128), F32)
        for g in range(per):
            rows = wide_rest[g * high : (g + 1) * high]
            if rows.shape[0] < high:
                pad = jnp.zeros((high - rows.shape[0], 128), F32)
                rows = jnp.concatenate([rows, pad], axis=0)
            folded = jnp.where(lane_group == g, rows, folded)
        return folded

    half = NZ // 2
    plan = (
        (term_of(gp0), zs0, zr0, 1),
        (term_of(gp1), zs1, zr1, -1),
        (term_of(gp2), zs2, zr2, 1),
        (rest_term, zs3, zr3, -1),
    )
    rings = []
    for term, sbuf, rbuf, way in plan:
        z_out = outgoing(sbuf.at[pl.ds(0, NZ - 1)])
        rings.append(((term, sbuf, rbuf, way, half, 0), z_out, []))
        rings.append(((term, sbuf, rbuf, -way, half - 1, half), z_out, []))

    def ring_step(ring, step):
        (term, sbuf, rbuf, way, length, base), z_out, got = ring
        if step >= length:
            return
        at = base + step
        value = term(way * (length - step))
        if step > 0:
            wait(got[-1], rbuf.at[at - 1])
            value = value + rbuf[at - 1].astype(F32)
        sbuf[at] = value.astype(BF)
        got.append(new())
        send(sbuf.at[at], rbuf.at[at], at_z(way), z_out, got[-1])

    def both_ways(piece, step):
        ring_step(rings[2 * piece], step)
        ring_step(rings[2 * piece + 1], step)

    wait(gp_in[0], gp0.at[inner])
    both_ways(0, 0)
    both_ways(3, 0)
    wait(gp_in[1], gp1.at[inner])
    both_ways(1, 0)
    wait(pg_in, pr_g)
    sg_out, sg_in = outgoing(sb_g), new()
    for at, k in enumerate(ways):
        main, tail = grad_sum(at)
        sb_g[at, :W] = main.astype(BF)
        sb_g[at, W:] = tail.astype(BF)
        send(sb_g.at[at], rb_g.at[at], at_y(k), sg_out, sg_in)
    both_ways(0, 1)
    both_ways(3, 1)
    wait(gp_in[2], gp2.at[inner])
    both_ways(2, 0)
    both_ways(1, 1)

    main = out_sum(3)
    wait(so_in, rb_o)
    for at in range(RING - 1):
        main = main + rb_o[at].astype(F32)
    tall[...] = jnp.zeros_like(tall)
    tall[:W] = main
    branch = jnp.transpose(tall[...])[:, :W]
    emb_v[...] = jnp.where(filled, placed_v[...] + scale_here * branch, 0.0).astype(BF)
    store_emb = pltpu.make_async_copy(emb_v, emb_out, osem.at[0])
    store_emb.start()

    both_ways(0, 2)
    both_ways(3, 2)
    both_ways(2, 1)
    both_ways(1, 2)

    main, tail = grad_sum(3)
    wait(sg_in, rb_g)
    for at in range(RING - 1):
        main = main + rb_g[at, :W].astype(F32)
        tail = tail + rb_g[at, W:].astype(F32)
    tall[:W] = main
    tall[W:XW] = tail * (radius * radius)
    upright = jnp.transpose(tall[...])
    mean_dot = upright[:, W : W + 1]
    grad_in = gain_here * upright[:, :W] - placed_v[...] * mean_dot
    tg_v[...] = jnp.where(filled, gm_v[...] + grad_in, 0.0).astype(BF)
    store_tg = pltpu.make_async_copy(tg_v, tg_out, osem.at[1])
    store_tg.start()

    both_ways(0, 3)
    both_ways(3, 3)
    both_ways(2, 2)
    both_ways(1, 3)

    def ring_end(piece):
        value = rings[2 * piece][0][0](0)
        for (_, _, rbuf, _, length, base), _, got in rings[2 * piece : 2 * piece + 2]:
            wait(got[-1], rbuf.at[base + length - 1])
            value = value + rbuf[base + length - 1].astype(F32)
        return value

    wg_v[:, :FP] = ring_end(0)[:CH].astype(BF)
    both_ways(2, 3)
    folded = ring_end(3)
    unfolded = [folded[:, g * FL : (g + 1) * FL] for g in range(per)]
    rest = jnp.concatenate(unfolded, axis=0)[:CH]
    wg_v[:, FP : FP + FL] = rest.astype(BF)
    wg_v[:, FP + FL : 2 * FP + FL] = ring_end(1)[:CH].astype(BF)
    wg_v[:, 2 * FP + FL :] = ring_end(2)[:CH].astype(BF)
    store_wg = pltpu.make_async_copy(wg_v, wg_out, osem.at[2])
    store_wg.start()

    for at, like in sent_later:
        wait(at, like)
    store_emb.wait()
    store_tg.wait()
    store_wg.wait()
    assert len(taken) == n_copies, len(taken)


def hand_over_kernel(a, b, c, a_out, b_out, c_out, a_v, b_v, c_v, sem):
    arrays = ((a, a_v, a_out), (b, b_v, b_out), (c, c_v, c_out))
    loads = [pltpu.make_async_copy(src, mid, sem.at[i]) for i, (src, mid, _) in enumerate(arrays)]
    stores = [pltpu.make_async_copy(mid, dst, sem.at[3 + i]) for i, (_, mid, dst) in enumerate(arrays)]
    for load in loads:
        load.start()
    for load, store in zip(loads, stores):
        load.wait()
        store.start()
    for store in stores:
        store.wait()


def hand_over(*arrays):
    hbm = pl.BlockSpec(memory_space=pl.ANY)
    return pl.pallas_call(
        hand_over_kernel,
        out_shape=tuple(jax.ShapeDtypeStruct(a.shape, a.dtype) for a in arrays),
        in_specs=[hbm] * 3,
        out_specs=(hbm,) * 3,
        scratch_shapes=[pltpu.VMEM(a.shape, a.dtype) for a in arrays]
        + [pltpu.SemaphoreType.DMA((6,))],
    )(*arrays)


def local(
    tiles, tile_counts, encoder_rank, out_grad, norm_gain, layer_scale, up_weight, down_weight
):
    slots, rows, width = tiles.shape
    ff = up_weight.shape[1]
    s = make_sizes(lax.axis_size("dp"), width, ff, slots, rows)
    NZ, W, F, T, DP = (s[k] for k in ("NZ", "W", "F", "T", "DP"))
    FP, FL, CB, CH, CP, XW, LW = (s[k] for k in ("FP", "FL", "CB", "CH", "CP", "XW", "LW"))
    D = W * 2 * RING
    n_copies = 66
    folded = (round_up(-(-CP // (128 // FL)), 16), 128)
    hbm = pl.BlockSpec(memory_space=pl.ANY)
    scratch = [
        pltpu.SMEM((DP * slots,), jnp.int32),
        pltpu.SMEM((DP * slots // 8,), jnp.int32),
        pltpu.VMEM((D,), F32),
        pltpu.VMEM((D,), F32),
        pltpu.VMEM((F, D), BF),
        pltpu.VMEM((F, D), BF),
        pltpu.VMEM((T, W), BF),
        pltpu.VMEM((T, W), BF),
        pltpu.VMEM((T, W), BF),
        pltpu.VMEM((T, W), BF),
        pltpu.VMEM((CH, F), BF),
        pltpu.VMEM((DP, rows, W), BF),
        pltpu.VMEM((DP, rows, W), BF),
        pltpu.VMEM((D, T), BF),
        pltpu.VMEM((D, T), BF),
        pltpu.VMEM((2, 8, T), F32),
        pltpu.VMEM((RING, 8, T), F32),
        pltpu.VMEM((T, LW), F32),
        pltpu.VMEM((LW, T), F32),
        pltpu.VMEM((T, W), F32),
        pltpu.VMEM((T, W), F32),
        pltpu.VMEM((F, T), BF),
        pltpu.VMEM((F, T), BF),
        pltpu.VMEM((F, T), F32),
        pltpu.VMEM((D, T), F32),
        pltpu.VMEM((D, T), F32),
        pltpu.VMEM((CB * CP, W), BF),
        pltpu.VMEM((RING - 1, CP, T), BF),
        pltpu.VMEM((RING, 2 * CB, CP, T), BF),
        pltpu.VMEM((RING, FP + FL, T), BF),
        pltpu.VMEM((RING, FP, T), BF),
        pltpu.VMEM((RING, FP, T), BF),
        pltpu.VMEM((4, W, T), BF),
        pltpu.VMEM((4, W, T), BF),
        pltpu.VMEM((3, W, T), BF),
        pltpu.VMEM((3, W, T), BF),
        pltpu.VMEM((4, XW, T), BF),
        pltpu.VMEM((4, XW, T), BF),
        pltpu.VMEM((3, XW, T), BF),
        pltpu.VMEM((3, XW, T), BF),
    ]
    for _ in range(6):
        scratch.append(pltpu.VMEM((NZ, CP, FP), BF))
    for _ in range(2):
        scratch.append(pltpu.VMEM((NZ,) + folded, BF))
    scratch += [
        pltpu.SemaphoreType.DMA((8,)),
        pltpu.SemaphoreType.DMA((3,)),
        pltpu.SemaphoreType.DMA((n_copies,)),
    ]
    emb, tg, wg = pl.pallas_call(
        functools.partial(kernel, s, n_copies),
        out_shape=(
            jax.ShapeDtypeStruct((T, W), BF),
            jax.ShapeDtypeStruct((T, W), BF),
            jax.ShapeDtypeStruct((CH, F), BF),
        ),
        in_specs=[hbm] * 8,
        out_specs=(hbm, hbm, hbm),
        scratch_shapes=scratch,
        compiler_params=pltpu.CompilerParams(
            collective_id=0, has_side_effects=True, vmem_limit_bytes=56 * 2**20
        ),
    )(
        encoder_rank,
        tile_counts,
        tiles.reshape(T, W),
        out_grad.reshape(T, W),
        norm_gain,
        layer_scale,
        up_weight.T,
        down_weight.T,
    )
    emb, tg, wg = hand_over(emb, tg, wg)
    return emb.reshape(tiles.shape), tg.reshape(tiles.shape), wg


def solution(mesh):
    in_specs = (
        P("dp", None, "mp"),
        P(),
        P(),
        P("dp", None, "mp"),
        P(),
        P(),
        P(None, "mp"),
        P(None, "mp"),
    )
    out_specs = (P("dp", None, "mp"), P("dp", None, "mp"), P("dp", "mp"))
    return jax.shard_map(local, mesh=mesh, in_specs=in_specs, out_specs=out_specs, check_vma=False)
```

```python
import functools

import jax
import jax.numpy as jnp
from jax import lax
from jax.experimental import pallas as pl
from jax.experimental.pallas import tpu as pltpu
from jax.sharding import PartitionSpec as P

norm_eps = 1e-06
half_root = 0.7071067811865476
pdf_scale = 0.3989422804014327
RING = 4
BF = jnp.bfloat16
F32 = jnp.float32


def round_up(value, to):
    return -(-value // to) * to


def make_sizes(mesh_dp, width, ff, slots, rows):
    s = {}
    s["NZ"] = mesh_dp // RING
    s["W"] = width
    s["F"] = ff
    s["SLOTS"] = slots
    s["R"] = rows
    s["T"] = slots * rows
    s["DP"] = mesh_dp
    s["FP"] = ff // 3 // 128 * 128
    s["FL"] = ff - 3 * s["FP"]
    s["CB"] = s["NZ"] // 2
    s["CH"] = width // s["CB"]
    s["CP"] = round_up(s["CH"], 8)
    s["XW"] = width + 16
    s["LW"] = round_up(width + 16, 128)
    return s


def first_dims(left, right):
    return lax.dot_general(left, right, (((0,), (0,)), ((), ())), preferred_element_type=F32)


def last_dims(left, right):
    return lax.dot_general(left, right, (((1,), (1,)), ((), ())), preferred_element_type=F32)


def grid_of(shape, axis):
    return lax.broadcasted_iota(jnp.int32, shape, axis)


def kernel(
    s, n_copies,
    enc_hbm, cnt_hbm, tiles_hbm, grad_hbm, gain_hbm, scale_hbm, up_hbm, down_hbm,
    emb_out, tg_out, wg_out,
    enc, cnt, gain, scale, up_v, down_v, tiles, out_grad, emb_v, tg_v, wg_v,
    out1, in1, g_all, x_all, sq_pair, sq_ring, wide, tall, placed_v, gm_v,
    hid_v, gpr_v, gh_v, acc_v, out_t, grad_t, sel_v, px, xq, gp0, gp1, gp2,
    ps_o, pr_o, sb_o, rb_o, ps_g, pr_g, sb_g, rb_g,
    xl_v, zt0, zt1, zt2, zt3, zs0, zr0, zs1, zr1, zs2, zr2, zs3, zr3,
    wsem, osem, sems,
):
    NZ, W, F, SLOTS, R, T, DP = (s[k] for k in ("NZ", "W", "F", "SLOTS", "R", "T", "DP"))
    FP, FL, CB, CH, CP, XW, LW = (s[k] for k in ("FP", "FL", "CB", "CH", "CP", "XW", "LW"))
    D = W * 2 * RING
    dp = lax.axis_index("dp")
    mp = lax.axis_index("mp")
    x, z = dp // NZ, dp % NZ
    y, c = mp // 2, mp % 2
    other = 1 - c

    def at_x(k):
        return {"dp": (x + k + RING) % RING * NZ + z, "mp": mp}

    def at_z(k):
        return {"dp": x * NZ + (z + k + NZ) % NZ, "mp": mp}

    def at_xz(i, k):
        return {"dp": (x + i) % RING * NZ + (z + k) % NZ, "mp": mp}

    def at_y(k):
        return {"dp": dp, "mp": (y + k + RING) % RING * 2 + c}

    partner = {"dp": dp, "mp": y * 2 + other}
    taken = []
    sent_later = []

    def new():
        taken.append(len(taken))
        return taken[-1]

    def send(src, dst, device, sent, got):
        copy = pltpu.make_async_remote_copy(
            src_ref=src, dst_ref=dst, send_sem=sems.at[sent], recv_sem=sems.at[got],
            device_id=device, device_id_type=pl.DeviceIdType.MESH,
        )
        copy.start()

    def wait(at, like):
        pltpu.make_async_copy(like, like, sems.at[at]).wait()

    def outgoing(like):
        at = new()
        sent_later.append((at, like))
        return at

    smalls = []
    for at, (src, dst) in enumerate(
        ((enc_hbm, enc), (cnt_hbm, cnt), (gain_hbm, gain), (scale_hbm, scale))
    ):
        smalls.append(pltpu.make_async_copy(src, dst, wsem.at[4 + at]))
    first = pltpu.make_async_copy(tiles_hbm, tiles, wsem.at[0])
    second = pltpu.make_async_copy(grad_hbm, out_grad, wsem.at[1])
    for small in smalls[:2] + [first] + smalls[2:] + [second]:
        small.start()

    barrier = pltpu.get_barrier_semaphore()
    others = [(i, k) for k in range(NZ) for i in range(RING) if (i, k) != (0, 0)]
    others.sort(key=lambda ik: -min(ik[0], RING - ik[0]) - min(ik[1], NZ - ik[1]))
    peers = [at_xz(i, k) for i, k in others]
    peers += [at_y(1), at_y(2), at_y(3), partner]
    for device in peers:
        pl.semaphore_signal(barrier, inc=1, device_id=device, device_id_type=pl.DeviceIdType.MESH)

    load_down = pltpu.make_async_copy(down_hbm, down_v, wsem.at[2])
    load_down.start()
    load_up = pltpu.make_async_copy(up_hbm, up_v, wsem.at[3])
    load_up.start()

    def block(j):
        return pl.ds(pl.multiple_of(j * W, 16), W)

    def part(j, lo, size):
        return pl.ds(pl.multiple_of(j * W + lo, 16), size)

    lane = grid_of((1, T), 1)
    smalls[0].wait()
    smalls[1].wait()
    dest = jnp.full((1, T), -1, jnp.int32)
    for j in range(SLOTS):
        live = (j % 8) < cnt[dp * (SLOTS // 8) + j // 8]
        goes = jnp.where(live, enc[dp * SLOTS + j], -1)
        dest = jnp.where((lane // R) == j, goes, dest)
    rows_all = DP * R
    row = grid_of((rows_all, T), 0)
    picker = ((row // R) == dest) & ((row % R) == (grid_of((rows_all, T), 1) % R))
    first.wait()
    picked = jnp.dot(picker.astype(BF), tiles[...], preferred_element_type=F32)
    out1[...] = picked.reshape(DP, R, W).astype(BF)

    pl.semaphore_wait(barrier, len(peers))
    ex_out, ex_in = outgoing(out1.at[pl.ds(0, DP - 1)]), new()
    for i, k in others:
        there = (x + i) % RING * NZ + (z + k) % NZ
        send(out1.at[there], in1.at[dp], at_xz(i, k), ex_out, ex_in)
    in1[dp] = out1[dp]

    lane_all = grid_of((1, rows_all), 1) // R

    def look(source, carry):
        count, order = carry
        comes = jnp.int32(0)
        for j in range(SLOTS):
            live = (j % 8) < cnt[source * (SLOTS // 8) + j // 8]
            here = enc[source * SLOTS + j] == dp
            comes = comes | (here.astype(jnp.int32) * live.astype(jnp.int32))
        order = jnp.where(
            lane_all == source, jnp.where(comes > 0, count, jnp.int32(SLOTS)), order
        )
        return count + comes, order

    count, order = lax.fori_loop(
        0, DP, look, (jnp.int32(0), jnp.full((1, rows_all), SLOTS, jnp.int32))
    )
    filled = (grid_of((T, 1), 0) // R) < count

    def local_part(ref):
        whole = ref[...].reshape(1, D)
        part = jnp.zeros((1, W), F32)
        for j in range(2 * RING):
            part = jnp.where(mp == j, whole[:, j * W : (j + 1) * W], part)
        return part

    smalls[2].wait()
    smalls[3].wait()
    gain_here = local_part(gain)
    scale_here = local_part(scale)

    second.wait()
    masked = jnp.where(filled, out_grad[...].astype(F32), 0.0)
    gm_v[...] = masked
    wide[...] = jnp.zeros_like(wide)
    wide[:, :W] = masked * scale_here
    g_all[block(mp)] = jnp.transpose(wide[...])[:W].astype(BF)

    ways = (2, 1, 3)

    seven = pl.ds(0, 7 * W)
    four = pl.ds(0, 4 * W)
    three = pl.ds(0, 3 * W)
    one = pl.ds(0, W)
    inner = pl.ds(1, RING - 1)

    def gather_1(buf, sent, pair, along):
        own = buf.at[block(mp)]
        send(own, own, partner, sent, pair)
        for k in ways:
            send(own, own, at_y(k), sent, along[k])

    def gather_2(buf, k, sent, pair):
        piece = buf.at[block((y - k + RING) % RING * 2 + c)]
        send(piece, piece, partner, sent, pair)

    g_out, g_pair, g_along = outgoing(g_all.at[seven]), new(), new()
    gather_1(g_all, g_out, g_pair, {k: g_along for k in ways})

    pack_row = grid_of((T, rows_all), 0)
    packer = ((pack_row // R) == order) & (
        (pack_row % R) == (grid_of((T, rows_all), 1) % R)
    )
    packer = packer.astype(BF)
    sel_row = grid_of((CB * CP, W), 0)
    sel_col = grid_of((CB * CP, W), 1)
    sel = jnp.zeros((CB * CP, W), jnp.bool_)
    for k in range(CB):
        sel = sel | (
            (sel_row - k * CP == sel_col - k * CH)
            & (sel_row >= k * CP)
            & (sel_row < k * CP + CH)
        )
    sel_v[...] = sel.astype(BF)
    sel_row = grid_of((CP, W), 0)
    sel_y = ((sel_row + y * CH) == grid_of((CP, W), 1)) & (sel_row < CH)
    sel_y = sel_y.astype(BF)

    wait(ex_in, in1.at[pl.ds(0, DP - 1)])
    arrived = in1[...].astype(F32).reshape(rows_all, W).astype(BF)
    placed = jnp.dot(packer, arrived, preferred_element_type=F32)
    placed_v[...] = placed
    wide[:, :W] = placed * gain_here
    x_all[block(mp)] = jnp.transpose(wide[...])[:W].astype(BF)
    x_out, x_pair = outgoing(x_all.at[seven]), new()
    x_along = {k: new() for k in ways}
    gather_1(x_all, x_out, x_pair, x_along)
    wide[:, :W] = placed * placed
    squares = jnp.sum(jnp.transpose(wide[...]), axis=0, keepdims=True)
    sq_pair[0] = jnp.broadcast_to(squares, (8, T))
    sq_got = new()
    send(sq_pair.at[0], sq_pair.at[1], partner, outgoing(sq_pair.at[0]), sq_got)

    mine = pl.ds(c * CB, CB)
    theirs = pl.ds(other * CB, CB)

    def quarter(j):
        moved = jnp.dot(sel_v[...], x_all[block(j)], preferred_element_type=F32)
        return moved.reshape(CB, CP, T).astype(BF)

    wait(g_along, g_all.at[three])
    for k in ways:
        gather_2(g_all, k, g_out, g_pair)
    wait(g_pair, g_all.at[four])
    load_down.wait()
    gh_v[...] = jnp.dot(down_v[...], g_all[...], preferred_element_type=F32)
    wait(sq_got, sq_pair.at[0])
    sq_ring[0] = sq_pair[0] + sq_pair[1]
    sq_out, sq_in = outgoing(sq_ring.at[inner]), new()
    for k in ways:
        send(sq_ring.at[0], sq_ring.at[k], at_y(k), sq_out, sq_in)

    for k in ways:
        wait(x_along[k], x_all.at[one])
        gather_2(x_all, k, x_out, x_pair)
    for parity in range(2):

        @pl.when(c == parity)
        def _():
            for at in range(RING):
                lo = (2 * at + parity) * W
                moved = jnp.dot(sel_y, x_all[lo : lo + W], preferred_element_type=F32)
                px[at] = moved.astype(BF)

    part_y = c * CB + y
    xq_out, xq_in = outgoing(px.at[pl.ds(0, RING - 1)]), new()
    for way in ways:
        send(px.at[(x + way) % RING], xq.at[way, part_y], at_x(way), xq_out, xq_in)
    load_up.wait()
    wait(x_pair, x_all.at[four])
    wait(sq_in, sq_ring.at[inner])
    total = sq_ring[0] + sq_ring[1] + sq_ring[2] + sq_ring[3]
    radius = lax.rsqrt(total[:1] / D + norm_eps)

    def through(buf, lo, hi):
        raw = acc_v[lo:hi]
        pre = radius * raw
        cdf = 0.5 * (1.0 + lax.erf(pre * half_root))
        slope = cdf + pre * jnp.exp(-0.5 * pre * pre) * pdf_scale
        hid_v[lo:hi] = (pre * cdf).astype(BF)
        back = radius * (gh_v[lo:hi] * slope)
        short = back.astype(BF)
        buf[0] = short
        gpr_v[lo:hi] = short
        sent, got = outgoing(buf.at[inner]), new()
        for k in ways:
            send(buf.at[0], buf.at[k], at_x(k), sent, got)
        return got, jnp.sum(back * raw, axis=0, keepdims=True)

    acc_v[...] = jnp.dot(up_v[...], x_all[...], preferred_element_type=F32)
    gp_in = []
    dots = jnp.zeros((1, T), F32)
    for buf, lo, hi in ((gp0, 0, FP + FL), (gp1, FP + FL, 2 * FP + FL), (gp2, 2 * FP + FL, F)):
        got, dot = through(buf, lo, hi)
        gp_in.append(got)
        dots = dots + dot
    dots = jnp.broadcast_to(dots / D, (16, T))
    wait(xq_in, px.at[pl.ds(0, RING - 1)])
    share_out, share_in = outgoing(xq.at[inner, mine]), new()
    piece = xq.at[inner, part_y]
    send(piece, piece, partner, share_out, share_in)
    xq_y_out = outgoing(xq.at[inner, inner])
    xq_y_in = {k: new() for k in ways}
    for k in ways:
        send(piece, piece, at_y(k), xq_y_out, xq_y_in[k])
    xq[0, mine] = quarter(x * 2 + c)
    xq[0, theirs] = quarter(x * 2 + other)

    out_t[...] = first_dims(down_v[...], hid_v[...])

    def block_of(k, core):
        return (y + k + RING) % RING * 2 + core

    def out_term(k, core):
        return out_t[block(block_of(k, core))]

    def grad_term(k, core):
        return grad_t[block(block_of(k, core))]

    order = (2, 1, 3, 0)
    po_out, po_in = outgoing(ps_o), new()
    for at, k in enumerate(order):
        ps_o[at] = out_term(k, other).astype(BF)
        send(ps_o.at[at], pr_o.at[at], partner, po_out, po_in)

    grad_t[...] = first_dims(up_v[...], gpr_v[...])
    pg_out, pg_in = outgoing(ps_g), new()
    for at, k in enumerate(order):
        ps_g[at, :W] = grad_term(k, other).astype(BF)
        ps_g[at, W:] = dots.astype(BF)
        send(ps_g.at[at], pr_g.at[at], partner, pg_out, pg_in)

    def out_sum(at):
        return out_term(order[at], c) + pr_o[at].astype(F32)

    def grad_sum(at):
        both = pr_g[at].astype(F32)
        return grad_term(order[at], c) + both[:W], dots + both[W:]

    wait(po_in, pr_o)
    so_out, so_in = outgoing(sb_o), new()
    for at, k in enumerate(ways):
        sb_o[at] = out_sum(at).astype(BF)
        send(sb_o.at[at], rb_o.at[at], at_y(k), so_out, so_in)

    for k in (1, 3, 2):
        piece = xq.at[inner, c * CB + (y - k + RING) % RING]
        wait(xq_y_in[k], piece)
        send(piece, piece, partner, share_out, share_in)
    wait(share_in, xq.at[inner, theirs])

    for k in range(NZ):
        xl_v[k * CP : (k + 1) * CP] = jnp.concatenate([xq[r, k] for r in range(RING)], axis=1)

    def turned(buf, lo, hi):
        return jnp.concatenate([buf[r, lo:hi] for r in range(RING)], axis=1)

    def terms(right, into):
        into[...] = last_dims(xl_v[...], right).reshape(NZ, CP, right.shape[0])

    def term_of(into):
        return lambda k: into[(z + k + NZ) % NZ]

    per = 128 // FL
    high = round_up(-(-CP // per), 16)
    lane_group = grid_of((high, 128), 1) // FL

    def rest_term(k):
        wide_rest = zt3[(z + k + NZ) % NZ]
        folded = jnp.zeros((high, 128), F32)
        for g in range(per):
            rows = wide_rest[g * high : (g + 1) * high]
            if rows.shape[0] < high:
                pad = jnp.zeros((high - rows.shape[0], 128), F32)
                rows = jnp.concatenate([rows, pad], axis=0)
            folded = jnp.where(lane_group == g, rows, folded)
        return folded

    half = NZ // 2
    plan = (
        (term_of(zt0), zs0, zr0, 1),
        (term_of(zt1), zs1, zr1, -1),
        (term_of(zt2), zs2, zr2, 1),
        (rest_term, zs3, zr3, -1),
    )
    rings = []
    for term, sbuf, rbuf, way in plan:
        z_out = outgoing(sbuf.at[pl.ds(0, NZ - 1)])
        rings.append(((term, sbuf, rbuf, way, half, 0), z_out, []))
        rings.append(((term, sbuf, rbuf, -way, half - 1, half), z_out, []))

    def ring_step(ring, step):
        (term, sbuf, rbuf, way, length, base), z_out, got = ring
        if step >= length:
            return
        at = base + step
        value = term(way * (length - step))
        if step > 0:
            wait(got[-1], rbuf.at[at - 1])
            value = value + rbuf[at - 1].astype(F32)
        sbuf[at] = value.astype(BF)
        got.append(new())
        send(sbuf.at[at], rbuf.at[at], at_z(way), z_out, got[-1])

    def both_ways(piece, step):
        ring_step(rings[2 * piece], step)
        ring_step(rings[2 * piece + 1], step)

    wait(gp_in[0], gp0.at[inner])
    terms(turned(gp0, 0, FP), zt0)
    both_ways(0, 0)
    terms(jnp.concatenate([turned(gp0, FP, FP + FL)] * per, axis=0), zt3)
    both_ways(3, 0)
    wait(gp_in[1], gp1.at[inner])
    terms(turned(gp1, 0, FP), zt1)
    both_ways(1, 0)
    wait(pg_in, pr_g)
    sg_out, sg_in = outgoing(sb_g), new()
    for at, k in enumerate(ways):
        main, tail = grad_sum(at)
        sb_g[at, :W] = main.astype(BF)
        sb_g[at, W:] = tail.astype(BF)
        send(sb_g.at[at], rb_g.at[at], at_y(k), sg_out, sg_in)
    both_ways(0, 1)
    both_ways(3, 1)
    wait(gp_in[2], gp2.at[inner])
    terms(turned(gp2, 0, FP), zt2)
    both_ways(2, 0)
    both_ways(1, 1)
    both_ways(0, 2)
    both_ways(3, 2)
    both_ways(2, 1)
    both_ways(1, 2)
    both_ways(0, 3)
    both_ways(3, 3)
    both_ways(2, 2)
    both_ways(1, 3)
    both_ways(2, 3)

    main = out_sum(3)
    wait(so_in, rb_o)
    for at in range(RING - 1):
        main = main + rb_o[at].astype(F32)
    tall[...] = jnp.zeros_like(tall)
    tall[:W] = main
    branch = jnp.transpose(tall[...])[:, :W]
    emb_v[...] = jnp.where(filled, placed_v[...] + scale_here * branch, 0.0).astype(BF)
    store_emb = pltpu.make_async_copy(emb_v, emb_out, osem.at[0])
    store_emb.start()

    main, tail = grad_sum(3)
    wait(sg_in, rb_g)
    for at in range(RING - 1):
        main = main + rb_g[at, :W].astype(F32)
        tail = tail + rb_g[at, W:].astype(F32)
    tall[:W] = main
    tall[W:XW] = tail * (radius * radius)
    upright = jnp.transpose(tall[...])
    mean_dot = upright[:, W : W + 1]
    grad_in = gain_here * upright[:, :W] - placed_v[...] * mean_dot
    tg_v[...] = jnp.where(filled, gm_v[...] + grad_in, 0.0).astype(BF)
    store_tg = pltpu.make_async_copy(tg_v, tg_out, osem.at[1])
    store_tg.start()

    def ring_end(piece):
        value = rings[2 * piece][0][0](0)
        for (_, _, rbuf, _, length, base), _, got in rings[2 * piece : 2 * piece + 2]:
            wait(got[-1], rbuf.at[base + length - 1])
            value = value + rbuf[base + length - 1].astype(F32)
        return value

    wg_v[:, :FP] = ring_end(0)[:CH].astype(BF)
    folded = ring_end(3)
    unfolded = [folded[:, g * FL : (g + 1) * FL] for g in range(per)]
    rest = jnp.concatenate(unfolded, axis=0)[:CH]
    wg_v[:, FP : FP + FL] = rest.astype(BF)
    wg_v[:, FP + FL : 2 * FP + FL] = ring_end(1)[:CH].astype(BF)
    wg_v[:, 2 * FP + FL :] = ring_end(2)[:CH].astype(BF)
    store_wg = pltpu.make_async_copy(wg_v, wg_out, osem.at[2])
    store_wg.start()

    for at, like in sent_later:
        wait(at, like)
    store_emb.wait()
    store_tg.wait()
    store_wg.wait()
    assert len(taken) == n_copies, len(taken)


def hand_over_kernel(a, b, c, a_out, b_out, c_out, a_v, b_v, c_v, sem):
    arrays = ((a, a_v, a_out), (b, b_v, b_out), (c, c_v, c_out))
    loads = [pltpu.make_async_copy(src, mid, sem.at[i]) for i, (src, mid, _) in enumerate(arrays)]
    stores = [pltpu.make_async_copy(mid, dst, sem.at[3 + i]) for i, (_, mid, dst) in enumerate(arrays)]
    for load in loads:
        load.start()
    for load, store in zip(loads, stores):
        load.wait()
        store.start()
    for store in stores:
        store.wait()


def hand_over(*arrays):
    hbm = pl.BlockSpec(memory_space=pl.ANY)
    return pl.pallas_call(
        hand_over_kernel,
        out_shape=tuple(jax.ShapeDtypeStruct(a.shape, a.dtype) for a in arrays),
        in_specs=[hbm] * 3,
        out_specs=(hbm,) * 3,
        scratch_shapes=[pltpu.VMEM(a.shape, a.dtype) for a in arrays]
        + [pltpu.SemaphoreType.DMA((6,))],
    )(*arrays)


def local(
    tiles, tile_counts, encoder_rank, out_grad, norm_gain, layer_scale, up_weight, down_weight
):
    slots, rows, width = tiles.shape
    ff = up_weight.shape[1]
    s = make_sizes(lax.axis_size("dp"), width, ff, slots, rows)
    NZ, W, F, T, DP = (s[k] for k in ("NZ", "W", "F", "T", "DP"))
    FP, FL, CB, CH, CP, XW, LW = (s[k] for k in ("FP", "FL", "CB", "CH", "CP", "XW", "LW"))
    D = W * 2 * RING
    n_copies = 68
    folded = (round_up(-(-CP // (128 // FL)), 16), 128)
    hbm = pl.BlockSpec(memory_space=pl.ANY)
    scratch = [
        pltpu.SMEM((DP * slots,), jnp.int32),
        pltpu.SMEM((DP * slots // 8,), jnp.int32),
        pltpu.VMEM((D,), F32),
        pltpu.VMEM((D,), F32),
        pltpu.VMEM((F, D), BF),
        pltpu.VMEM((F, D), BF),
        pltpu.VMEM((T, W), BF),
        pltpu.VMEM((T, W), BF),
        pltpu.VMEM((T, W), BF),
        pltpu.VMEM((T, W), BF),
        pltpu.VMEM((CH, F), BF),
        pltpu.VMEM((DP, rows, W), BF),
        pltpu.VMEM((DP, rows, W), BF),
        pltpu.VMEM((D, T), BF),
        pltpu.VMEM((D, T), BF),
        pltpu.VMEM((2, 8, T), F32),
        pltpu.VMEM((RING, 8, T), F32),
        pltpu.VMEM((T, LW), F32),
        pltpu.VMEM((LW, T), F32),
        pltpu.VMEM((T, W), F32),
        pltpu.VMEM((T, W), F32),
        pltpu.VMEM((F, T), BF),
        pltpu.VMEM((F, T), BF),
        pltpu.VMEM((F, T), F32),
        pltpu.VMEM((F, T), F32),
        pltpu.VMEM((D, T), F32),
        pltpu.VMEM((D, T), F32),
        pltpu.VMEM((CB * CP, W), BF),
        pltpu.VMEM((RING, CP, T), BF),
        pltpu.VMEM((RING, 2 * CB, CP, T), BF),
        pltpu.VMEM((RING, FP + FL, T), BF),
        pltpu.VMEM((RING, FP, T), BF),
        pltpu.VMEM((RING, FP, T), BF),
        pltpu.VMEM((4, W, T), BF),
        pltpu.VMEM((4, W, T), BF),
        pltpu.VMEM((3, W, T), BF),
        pltpu.VMEM((3, W, T), BF),
        pltpu.VMEM((4, XW, T), BF),
        pltpu.VMEM((4, XW, T), BF),
        pltpu.VMEM((3, XW, T), BF),
        pltpu.VMEM((3, XW, T), BF),
    ]
    scratch.append(pltpu.VMEM((NZ * CP, RING * T), BF))
    scratch += [pltpu.VMEM((NZ, CP, FP), F32) for _ in range(3)]
    scratch.append(pltpu.VMEM((NZ, CP, 128), F32))
    for _ in range(6):
        scratch.append(pltpu.VMEM((NZ, CP, FP), BF))
    for _ in range(2):
        scratch.append(pltpu.VMEM((NZ,) + folded, BF))
    scratch += [
        pltpu.SemaphoreType.DMA((8,)),
        pltpu.SemaphoreType.DMA((3,)),
        pltpu.SemaphoreType.DMA((n_copies,)),
    ]
    emb, tg, wg = pl.pallas_call(
        functools.partial(kernel, s, n_copies),
        out_shape=(
            jax.ShapeDtypeStruct((T, W), BF),
            jax.ShapeDtypeStruct((T, W), BF),
            jax.ShapeDtypeStruct((CH, F), BF),
        ),
        in_specs=[hbm] * 8,
        out_specs=(hbm, hbm, hbm),
        scratch_shapes=scratch,
        compiler_params=pltpu.CompilerParams(
            collective_id=0, has_side_effects=True, vmem_limit_bytes=56 * 2**20
        ),
    )(
        encoder_rank,
        tile_counts,
        tiles.reshape(T, W),
        out_grad.reshape(T, W),
        norm_gain,
        layer_scale,
        up_weight.T,
        down_weight.T,
    )
    emb, tg, wg = hand_over(emb, tg, wg)
    return emb.reshape(tiles.shape), tg.reshape(tiles.shape), wg


def solution(mesh):
    in_specs = (
        P("dp", None, "mp"),
        P(),
        P(),
        P("dp", None, "mp"),
        P(),
        P(),
        P(None, "mp"),
        P(None, "mp"),
    )
    out_specs = (P("dp", None, "mp"), P("dp", None, "mp"), P("dp", "mp"))
    return jax.shard_map(local, mesh=mesh, in_specs=in_specs, out_specs=out_specs, check_vma=False)
```

```python
import functools

import jax
import jax.numpy as jnp
from jax import lax
from jax.experimental import pallas as pl
from jax.experimental.pallas import tpu as pltpu
from jax.sharding import PartitionSpec as P

norm_eps = 1e-06
half_root = 0.7071067811865476
pdf_scale = 0.3989422804014327
RING = 4
BF = jnp.bfloat16
F32 = jnp.float32


def round_up(value, to):
    return -(-value // to) * to


def make_sizes(mesh_dp, width, ff, slots, rows):
    s = {}
    s["NZ"] = mesh_dp // RING
    s["W"] = width
    s["F"] = ff
    s["SLOTS"] = slots
    s["R"] = rows
    s["T"] = slots * rows
    s["DP"] = mesh_dp
    s["FP"] = ff // 3 // 128 * 128
    s["FL"] = ff - 3 * s["FP"]
    s["CB"] = s["NZ"] // 2
    s["CH"] = width // s["CB"]
    s["CP"] = round_up(s["CH"], 8)
    s["XW"] = width + 16
    s["LW"] = round_up(width + 16, 128)
    return s


def first_dims(left, right):
    return lax.dot_general(left, right, (((0,), (0,)), ((), ())), preferred_element_type=F32)


def last_dims(left, right):
    return lax.dot_general(left, right, (((1,), (1,)), ((), ())), preferred_element_type=F32)


def grid_of(shape, axis):
    return lax.broadcasted_iota(jnp.int32, shape, axis)


def kernel(
    s, n_copies,
    enc_hbm, cnt_hbm, tiles_hbm, grad_hbm, gain_hbm, scale_hbm, up_hbm, down_hbm,
    emb_out, tg_out, wg_out,
    enc, cnt, gain, scale, up_v, down_v, tiles, out_grad, emb_v, tg_v, wg_v,
    out1, in1, g_all, x_all, sq_pair, sq_ring, wide, tall, placed_v, gm_v,
    hid_v, gpr_v, gh_v, acc_v, out_t, grad_t, sel_v, px, xq, gp0, gp1, gp2,
    ps_o, pr_o, sb_o, rb_o, ps_g, pr_g, sb_g, rb_g,
    xl_v, zt0, zt1, zt2, zt3, zs0, zr0, zs1, zr1, zs2, zr2, zs3, zr3,
    wsem, osem, sems,
):
    NZ, W, F, SLOTS, R, T, DP = (s[k] for k in ("NZ", "W", "F", "SLOTS", "R", "T", "DP"))
    FP, FL, CB, CH, CP, XW, LW = (s[k] for k in ("FP", "FL", "CB", "CH", "CP", "XW", "LW"))
    D = W * 2 * RING
    dp = lax.axis_index("dp")
    mp = lax.axis_index("mp")
    x, z = dp // NZ, dp % NZ
    y, c = mp // 2, mp % 2
    other = 1 - c

    def at_x(k):
        return {"dp": (x + k + RING) % RING * NZ + z, "mp": mp}

    def at_z(k):
        return {"dp": x * NZ + (z + k + NZ) % NZ, "mp": mp}

    def at_xz(i, k):
        return {"dp": (x + i) % RING * NZ + (z + k) % NZ, "mp": mp}

    def at_y(k):
        return {"dp": dp, "mp": (y + k + RING) % RING * 2 + c}

    partner = {"dp": dp, "mp": y * 2 + other}
    taken = []
    sent_later = []

    def new():
        taken.append(len(taken))
        return taken[-1]

    def send(src, dst, device, sent, got):
        copy = pltpu.make_async_remote_copy(
            src_ref=src, dst_ref=dst, send_sem=sems.at[sent], recv_sem=sems.at[got],
            device_id=device, device_id_type=pl.DeviceIdType.MESH,
        )
        copy.start()

    def wait(at, like):
        pltpu.make_async_copy(like, like, sems.at[at]).wait()

    def outgoing(like):
        at = new()
        sent_later.append((at, like))
        return at

    smalls = []
    for at, (src, dst) in enumerate(
        ((enc_hbm, enc), (cnt_hbm, cnt), (gain_hbm, gain), (scale_hbm, scale))
    ):
        smalls.append(pltpu.make_async_copy(src, dst, wsem.at[4 + at]))
    first = pltpu.make_async_copy(tiles_hbm, tiles, wsem.at[0])
    second = pltpu.make_async_copy(grad_hbm, out_grad, wsem.at[1])
    for small in smalls[:2] + [first] + smalls[2:] + [second]:
        small.start()

    barrier = pltpu.get_barrier_semaphore()
    others = [(i, k) for k in range(NZ) for i in range(RING) if (i, k) != (0, 0)]
    others.sort(key=lambda ik: -min(ik[0], RING - ik[0]) - min(ik[1], NZ - ik[1]))
    peers = [at_xz(i, k) for i, k in others]
    peers += [at_y(1), at_y(2), at_y(3), partner]
    for device in peers:
        pl.semaphore_signal(barrier, inc=1, device_id=device, device_id_type=pl.DeviceIdType.MESH)

    load_down = pltpu.make_async_copy(down_hbm, down_v, wsem.at[2])
    load_down.start()
    load_up = pltpu.make_async_copy(up_hbm, up_v, wsem.at[3])
    load_up.start()

    def block(j):
        return pl.ds(pl.multiple_of(j * W, 16), W)

    def part(j, lo, size):
        return pl.ds(pl.multiple_of(j * W + lo, 16), size)

    lane = grid_of((1, T), 1)
    smalls[0].wait()
    smalls[1].wait()
    dest = jnp.full((1, T), -1, jnp.int32)
    for j in range(SLOTS):
        live = (j % 8) < cnt[dp * (SLOTS // 8) + j // 8]
        goes = jnp.where(live, enc[dp * SLOTS + j], -1)
        dest = jnp.where((lane // R) == j, goes, dest)
    rows_all = DP * R
    row = grid_of((rows_all, T), 0)
    picker = ((row // R) == dest) & ((row % R) == (grid_of((rows_all, T), 1) % R))
    first.wait()
    picked = jnp.dot(picker.astype(BF), tiles[...], preferred_element_type=F32)
    out1[...] = picked.reshape(DP, R, W).astype(BF)

    pl.semaphore_wait(barrier, len(peers))
    ex_out, ex_in = outgoing(out1.at[pl.ds(0, DP - 1)]), new()
    for i, k in others:
        there = (x + i) % RING * NZ + (z + k) % NZ
        send(out1.at[there], in1.at[dp], at_xz(i, k), ex_out, ex_in)
    in1[dp] = out1[dp]

    lane_all = grid_of((1, rows_all), 1) // R

    def look(source, carry):
        count, order = carry
        comes = jnp.int32(0)
        for j in range(SLOTS):
            live = (j % 8) < cnt[source * (SLOTS // 8) + j // 8]
            here = enc[source * SLOTS + j] == dp
            comes = comes | (here.astype(jnp.int32) * live.astype(jnp.int32))
        order = jnp.where(
            lane_all == source, jnp.where(comes > 0, count, jnp.int32(SLOTS)), order
        )
        return count + comes, order

    count, order = lax.fori_loop(
        0, DP, look, (jnp.int32(0), jnp.full((1, rows_all), SLOTS, jnp.int32))
    )
    filled = (grid_of((T, 1), 0) // R) < count

    def local_part(ref):
        whole = ref[...].reshape(1, D)
        part = jnp.zeros((1, W), F32)
        for j in range(2 * RING):
            part = jnp.where(mp == j, whole[:, j * W : (j + 1) * W], part)
        return part

    smalls[2].wait()
    smalls[3].wait()
    gain_here = local_part(gain)
    scale_here = local_part(scale)

    second.wait()
    masked = jnp.where(filled, out_grad[...].astype(F32), 0.0)
    gm_v[...] = masked
    wide[...] = jnp.zeros_like(wide)
    wide[:, :W] = masked * scale_here
    g_all[block(mp)] = jnp.transpose(wide[...])[:W].astype(BF)

    ways = (2, 1, 3)

    seven = pl.ds(0, 7 * W)
    four = pl.ds(0, 4 * W)
    three = pl.ds(0, 3 * W)
    one = pl.ds(0, W)
    inner = pl.ds(1, RING - 1)

    def gather_1(buf, sent, pair, along):
        own = buf.at[block(mp)]
        send(own, own, partner, sent, pair)
        for k in ways:
            send(own, own, at_y(k), sent, along[k])

    def gather_2(buf, k, sent, pair):
        piece = buf.at[block((y - k + RING) % RING * 2 + c)]
        send(piece, piece, partner, sent, pair)

    g_out, g_pair, g_along = outgoing(g_all.at[seven]), new(), new()
    gather_1(g_all, g_out, g_pair, {k: g_along for k in ways})

    pack_row = grid_of((T, rows_all), 0)
    packer = ((pack_row // R) == order) & (
        (pack_row % R) == (grid_of((T, rows_all), 1) % R)
    )
    packer = packer.astype(BF)
    sel_row = grid_of((CB * CP, W), 0)
    sel_col = grid_of((CB * CP, W), 1)
    sel = jnp.zeros((CB * CP, W), jnp.bool_)
    for k in range(CB):
        sel = sel | (
            (sel_row - k * CP == sel_col - k * CH)
            & (sel_row >= k * CP)
            & (sel_row < k * CP + CH)
        )
    sel_v[...] = sel.astype(BF)
    sel_row = grid_of((CP, W), 0)
    sel_y = ((sel_row + y * CH) == grid_of((CP, W), 1)) & (sel_row < CH)
    sel_y = sel_y.astype(BF)

    wait(ex_in, in1.at[pl.ds(0, DP - 1)])
    arrived = in1[...].astype(F32).reshape(rows_all, W).astype(BF)
    placed = jnp.dot(packer, arrived, preferred_element_type=F32)
    placed_v[...] = placed
    wide[:, :W] = placed * gain_here
    x_all[block(mp)] = jnp.transpose(wide[...])[:W].astype(BF)
    x_out, x_pair = outgoing(x_all.at[seven]), new()
    x_along = {k: new() for k in ways}
    gather_1(x_all, x_out, x_pair, x_along)
    wide[:, :W] = placed * placed
    squares = jnp.sum(jnp.transpose(wide[...]), axis=0, keepdims=True)
    sq_pair[0] = jnp.broadcast_to(squares, (8, T))
    sq_got = new()
    send(sq_pair.at[0], sq_pair.at[1], partner, outgoing(sq_pair.at[0]), sq_got)

    mine = pl.ds(c * CB, CB)
    theirs = pl.ds(other * CB, CB)

    def quarter(j):
        moved = jnp.dot(sel_v[...], x_all[block(j)], preferred_element_type=F32)
        return moved.reshape(CB, CP, T).astype(BF)

    wait(g_along, g_all.at[three])
    for k in ways:
        gather_2(g_all, k, g_out, g_pair)
    wait(g_pair, g_all.at[four])
    load_down.wait()
    gh_v[...] = jnp.dot(down_v[...], g_all[...], preferred_element_type=F32)
    wait(sq_got, sq_pair.at[0])
    sq_ring[0] = sq_pair[0] + sq_pair[1]
    sq_out, sq_in = outgoing(sq_ring.at[inner]), new()
    for k in ways:
        send(sq_ring.at[0], sq_ring.at[k], at_y(k), sq_out, sq_in)

    for k in ways:
        wait(x_along[k], x_all.at[one])
        gather_2(x_all, k, x_out, x_pair)
    for parity in range(2):

        @pl.when(c == parity)
        def _():
            starts = [(2 * at + parity) * W for at in range(RING)]
            rows = jnp.concatenate([x_all[lo : lo + W] for lo in starts], axis=1)
            moved = jnp.dot(sel_y, rows, preferred_element_type=F32).astype(BF)
            for at in range(RING):
                px[at] = moved[:, at * T : (at + 1) * T]

    part_y = c * CB + y
    xq_out = outgoing(px.at[pl.ds(0, RING - 1)])
    xq_in = {way: new() for way in ways}
    for way in ways:
        send(px.at[(x + way) % RING], xq.at[way, part_y], at_x(way), xq_out, xq_in[way])
    load_up.wait()
    wait(x_pair, x_all.at[four])
    wait(sq_in, sq_ring.at[inner])
    total = sq_ring[0] + sq_ring[1] + sq_ring[2] + sq_ring[3]
    radius = lax.rsqrt(total[:1] / D + norm_eps)

    def through(buf, lo, hi):
        raw = acc_v[lo:hi]
        pre = radius * raw
        cdf = 0.5 * (1.0 + lax.erf(pre * half_root))
        slope = cdf + pre * jnp.exp(-0.5 * pre * pre) * pdf_scale
        hid_v[lo:hi] = (pre * cdf).astype(BF)
        back = radius * (gh_v[lo:hi] * slope)
        short = back.astype(BF)
        buf[0] = short
        gpr_v[lo:hi] = short
        sent, got = outgoing(buf.at[inner]), new()
        for k in ways:
            send(buf.at[0], buf.at[k], at_x(k), sent, got)
        return got, jnp.sum(back * raw, axis=0, keepdims=True)

    acc_v[...] = jnp.dot(up_v[...], x_all[...], preferred_element_type=F32)
    gp_in = []
    dots = jnp.zeros((1, T), F32)
    for buf, lo, hi in ((gp0, 0, FP + FL), (gp1, FP + FL, 2 * FP + FL), (gp2, 2 * FP + FL, F)):
        got, dot = through(buf, lo, hi)
        gp_in.append(got)
        dots = dots + dot
    dots = jnp.broadcast_to(dots / D, (16, T))
    xq[0, mine] = quarter(x * 2 + c)
    xq[0, theirs] = quarter(x * 2 + other)
    share_out, share_in = outgoing(xq.at[inner, mine]), new()
    xq_y_out = outgoing(xq.at[inner, inner])
    xq_y_in = {k: new() for k in ways}
    for way in (1, 3, 2):
        piece = xq.at[way, part_y]
        wait(xq_in[way], piece)
        for k in ways:
            send(piece, piece, at_y(k), xq_y_out, xq_y_in[k])
    piece = xq.at[inner, part_y]
    send(piece, piece, partner, share_out, share_in)

    out_t[...] = first_dims(down_v[...], hid_v[...])

    def block_of(k, core):
        return (y + k + RING) % RING * 2 + core

    def out_term(k, core):
        return out_t[block(block_of(k, core))]

    def grad_term(k, core):
        return grad_t[block(block_of(k, core))]

    order = (2, 1, 3, 0)
    po_out, po_in = outgoing(ps_o), new()
    for at, k in enumerate(order):
        ps_o[at] = out_term(k, other).astype(BF)
        send(ps_o.at[at], pr_o.at[at], partner, po_out, po_in)

    grad_t[...] = first_dims(up_v[...], gpr_v[...])
    pg_out, pg_in = outgoing(ps_g), new()
    for at, k in enumerate(order):
        ps_g[at, :W] = grad_term(k, other).astype(BF)
        ps_g[at, W:] = dots.astype(BF)
        send(ps_g.at[at], pr_g.at[at], partner, pg_out, pg_in)

    def out_sum(at):
        return out_term(order[at], c) + pr_o[at].astype(F32)

    def grad_sum(at):
        both = pr_g[at].astype(F32)
        return grad_term(order[at], c) + both[:W], dots + both[W:]

    wait(po_in, pr_o)
    so_out, so_in = outgoing(sb_o), new()
    for at, k in enumerate(ways):
        sb_o[at] = out_sum(at).astype(BF)
        send(sb_o.at[at], rb_o.at[at], at_y(k), so_out, so_in)

    for k in (1, 3, 2):
        piece = xq.at[inner, c * CB + (y - k + RING) % RING]
        wait(xq_y_in[k], piece)
        send(piece, piece, partner, share_out, share_in)
    wait(share_in, xq.at[inner, theirs])

    for k in range(NZ):
        xl_v[k * CP : (k + 1) * CP] = jnp.concatenate([xq[r, k] for r in range(RING)], axis=1)

    def turned(buf, lo, hi):
        return jnp.concatenate([buf[r, lo:hi] for r in range(RING)], axis=1)

    def terms(right, into):
        into[...] = last_dims(xl_v[...], right).reshape(NZ, CP, right.shape[0])

    def term_of(into):
        return lambda k: into[(z + k + NZ) % NZ]

    per = 128 // FL
    high = round_up(-(-CP // per), 16)
    lane_group = grid_of((high, 128), 1) // FL

    def rest_term(k):
        wide_rest = zt3[(z + k + NZ) % NZ]
        folded = jnp.zeros((high, 128), F32)
        for g in range(per):
            rows = wide_rest[g * high : (g + 1) * high]
            if rows.shape[0] < high:
                pad = jnp.zeros((high - rows.shape[0], 128), F32)
                rows = jnp.concatenate([rows, pad], axis=0)
            folded = jnp.where(lane_group == g, rows, folded)
        return folded

    half = NZ // 2
    plan = (
        (term_of(zt0), zs0, zr0, 1),
        (term_of(zt1), zs1, zr1, -1),
        (term_of(zt2), zs2, zr2, 1),
        (rest_term, zs3, zr3, -1),
    )
    rings = []
    for term, sbuf, rbuf, way in plan:
        z_out = outgoing(sbuf.at[pl.ds(0, NZ - 1)])
        rings.append(((term, sbuf, rbuf, way, half, 0), z_out, []))
        rings.append(((term, sbuf, rbuf, -way, half - 1, half), z_out, []))

    def ring_step(ring, step):
        (term, sbuf, rbuf, way, length, base), z_out, got = ring
        if step >= length:
            return
        at = base + step
        value = term(way * (length - step))
        if step > 0:
            wait(got[-1], rbuf.at[at - 1])
            value = value + rbuf[at - 1].astype(F32)
        sbuf[at] = value.astype(BF)
        got.append(new())
        send(sbuf.at[at], rbuf.at[at], at_z(way), z_out, got[-1])

    def both_ways(piece, step):
        ring_step(rings[2 * piece], step)
        ring_step(rings[2 * piece + 1], step)

    wait(gp_in[0], gp0.at[inner])
    terms(turned(gp0, 0, FP), zt0)
    both_ways(0, 0)
    terms(jnp.concatenate([turned(gp0, FP, FP + FL)] * per, axis=0), zt3)
    both_ways(3, 0)
    wait(gp_in[1], gp1.at[inner])
    terms(turned(gp1, 0, FP), zt1)
    both_ways(1, 0)
    wait(pg_in, pr_g)
    sg_out, sg_in = outgoing(sb_g), new()
    for at, k in enumerate(ways):
        main, tail = grad_sum(at)
        sb_g[at, :W] = main.astype(BF)
        sb_g[at, W:] = tail.astype(BF)
        send(sb_g.at[at], rb_g.at[at], at_y(k), sg_out, sg_in)
    both_ways(0, 1)
    both_ways(3, 1)
    wait(gp_in[2], gp2.at[inner])
    terms(turned(gp2, 0, FP), zt2)
    both_ways(2, 0)
    both_ways(1, 1)
    both_ways(0, 2)
    both_ways(3, 2)
    both_ways(2, 1)
    both_ways(1, 2)
    both_ways(0, 3)
    both_ways(3, 3)
    both_ways(2, 2)
    both_ways(1, 3)
    both_ways(2, 3)

    main = out_sum(3)
    wait(so_in, rb_o)
    for at in range(RING - 1):
        main = main + rb_o[at].astype(F32)
    tall[...] = jnp.zeros_like(tall)
    tall[:W] = main
    branch = jnp.transpose(tall[...])[:, :W]
    emb_v[...] = jnp.where(filled, placed_v[...] + scale_here * branch, 0.0).astype(BF)
    store_emb = pltpu.make_async_copy(emb_v, emb_out, osem.at[0])
    store_emb.start()

    main, tail = grad_sum(3)
    wait(sg_in, rb_g)
    for at in range(RING - 1):
        main = main + rb_g[at, :W].astype(F32)
        tail = tail + rb_g[at, W:].astype(F32)
    tall[:W] = main
    tall[W:XW] = tail * (radius * radius)
    upright = jnp.transpose(tall[...])
    mean_dot = upright[:, W : W + 1]
    grad_in = gain_here * upright[:, :W] - placed_v[...] * mean_dot
    tg_v[...] = jnp.where(filled, gm_v[...] + grad_in, 0.0).astype(BF)
    store_tg = pltpu.make_async_copy(tg_v, tg_out, osem.at[1])
    store_tg.start()

    def ring_end(piece):
        value = rings[2 * piece][0][0](0)
        for (_, _, rbuf, _, length, base), _, got in rings[2 * piece : 2 * piece + 2]:
            wait(got[-1], rbuf.at[base + length - 1])
            value = value + rbuf[base + length - 1].astype(F32)
        return value

    wg_v[:, :FP] = ring_end(0)[:CH].astype(BF)
    folded = ring_end(3)
    unfolded = [folded[:, g * FL : (g + 1) * FL] for g in range(per)]
    rest = jnp.concatenate(unfolded, axis=0)[:CH]
    wg_v[:, FP : FP + FL] = rest.astype(BF)
    wg_v[:, FP + FL : 2 * FP + FL] = ring_end(1)[:CH].astype(BF)
    wg_v[:, 2 * FP + FL :] = ring_end(2)[:CH].astype(BF)
    store_wg = pltpu.make_async_copy(wg_v, wg_out, osem.at[2])
    store_wg.start()

    for at, like in sent_later:
        wait(at, like)
    store_emb.wait()
    store_tg.wait()
    store_wg.wait()
    assert len(taken) == n_copies, len(taken)


def hand_over_kernel(a, b, c, a_out, b_out, c_out, a_v, b_v, c_v, sem):
    arrays = ((a, a_v, a_out), (b, b_v, b_out), (c, c_v, c_out))
    loads = [pltpu.make_async_copy(src, mid, sem.at[i]) for i, (src, mid, _) in enumerate(arrays)]
    stores = [pltpu.make_async_copy(mid, dst, sem.at[3 + i]) for i, (_, mid, dst) in enumerate(arrays)]
    for load in loads:
        load.start()
    for load, store in zip(loads, stores):
        load.wait()
        store.start()
    for store in stores:
        store.wait()


def hand_over(*arrays):
    hbm = pl.BlockSpec(memory_space=pl.ANY)
    return pl.pallas_call(
        hand_over_kernel,
        out_shape=tuple(jax.ShapeDtypeStruct(a.shape, a.dtype) for a in arrays),
        in_specs=[hbm] * 3,
        out_specs=(hbm,) * 3,
        scratch_shapes=[pltpu.VMEM(a.shape, a.dtype) for a in arrays]
        + [pltpu.SemaphoreType.DMA((6,))],
    )(*arrays)


def local(
    tiles, tile_counts, encoder_rank, out_grad, norm_gain, layer_scale, up_weight, down_weight
):
    slots, rows, width = tiles.shape
    ff = up_weight.shape[1]
    s = make_sizes(lax.axis_size("dp"), width, ff, slots, rows)
    NZ, W, F, T, DP = (s[k] for k in ("NZ", "W", "F", "T", "DP"))
    FP, FL, CB, CH, CP, XW, LW = (s[k] for k in ("FP", "FL", "CB", "CH", "CP", "XW", "LW"))
    D = W * 2 * RING
    n_copies = 70
    folded = (round_up(-(-CP // (128 // FL)), 16), 128)
    hbm = pl.BlockSpec(memory_space=pl.ANY)
    scratch = [
        pltpu.SMEM((DP * slots,), jnp.int32),
        pltpu.SMEM((DP * slots // 8,), jnp.int32),
        pltpu.VMEM((D,), F32),
        pltpu.VMEM((D,), F32),
        pltpu.VMEM((F, D), BF),
        pltpu.VMEM((F, D), BF),
        pltpu.VMEM((T, W), BF),
        pltpu.VMEM((T, W), BF),
        pltpu.VMEM((T, W), BF),
        pltpu.VMEM((T, W), BF),
        pltpu.VMEM((CH, F), BF),
        pltpu.VMEM((DP, rows, W), BF),
        pltpu.VMEM((DP, rows, W), BF),
        pltpu.VMEM((D, T), BF),
        pltpu.VMEM((D, T), BF),
        pltpu.VMEM((2, 8, T), F32),
        pltpu.VMEM((RING, 8, T), F32),
        pltpu.VMEM((T, LW), F32),
        pltpu.VMEM((LW, T), F32),
        pltpu.VMEM((T, W), F32),
        pltpu.VMEM((T, W), F32),
        pltpu.VMEM((F, T), BF),
        pltpu.VMEM((F, T), BF),
        pltpu.VMEM((F, T), F32),
        pltpu.VMEM((F, T), F32),
        pltpu.VMEM((D, T), F32),
        pltpu.VMEM((D, T), F32),
        pltpu.VMEM((CB * CP, W), BF),
        pltpu.VMEM((RING, CP, T), BF),
        pltpu.VMEM((RING, 2 * CB, CP, T), BF),
        pltpu.VMEM((RING, FP + FL, T), BF),
        pltpu.VMEM((RING, FP, T), BF),
        pltpu.VMEM((RING, FP, T), BF),
        pltpu.VMEM((4, W, T), BF),
        pltpu.VMEM((4, W, T), BF),
        pltpu.VMEM((3, W, T), BF),
        pltpu.VMEM((3, W, T), BF),
        pltpu.VMEM((4, XW, T), BF),
        pltpu.VMEM((4, XW, T), BF),
        pltpu.VMEM((3, XW, T), BF),
        pltpu.VMEM((3, XW, T), BF),
    ]
    scratch.append(pltpu.VMEM((NZ * CP, RING * T), BF))
    scratch += [pltpu.VMEM((NZ, CP, FP), F32) for _ in range(3)]
    scratch.append(pltpu.VMEM((NZ, CP, 128), F32))
    for _ in range(6):
        scratch.append(pltpu.VMEM((NZ, CP, FP), BF))
    for _ in range(2):
        scratch.append(pltpu.VMEM((NZ,) + folded, BF))
    scratch += [
        pltpu.SemaphoreType.DMA((8,)),
        pltpu.SemaphoreType.DMA((3,)),
        pltpu.SemaphoreType.DMA((n_copies,)),
    ]
    emb, tg, wg = pl.pallas_call(
        functools.partial(kernel, s, n_copies),
        out_shape=(
            jax.ShapeDtypeStruct((T, W), BF),
            jax.ShapeDtypeStruct((T, W), BF),
            jax.ShapeDtypeStruct((CH, F), BF),
        ),
        in_specs=[hbm] * 8,
        out_specs=(hbm, hbm, hbm),
        scratch_shapes=scratch,
        compiler_params=pltpu.CompilerParams(
            collective_id=0, has_side_effects=True, vmem_limit_bytes=56 * 2**20
        ),
    )(
        encoder_rank,
        tile_counts,
        tiles.reshape(T, W),
        out_grad.reshape(T, W),
        norm_gain,
        layer_scale,
        up_weight.T,
        down_weight.T,
    )
    emb, tg, wg = hand_over(emb, tg, wg)
    return emb.reshape(tiles.shape), tg.reshape(tiles.shape), wg


def solution(mesh):
    in_specs = (
        P("dp", None, "mp"),
        P(),
        P(),
        P("dp", None, "mp"),
        P(),
        P(),
        P(None, "mp"),
        P(None, "mp"),
    )
    out_specs = (P("dp", None, "mp"), P("dp", None, "mp"), P("dp", "mp"))
    return jax.shard_map(local, mesh=mesh, in_specs=in_specs, out_specs=out_specs, check_vma=False)
```
